256 devices in a mesh: grp: 4 (over z_lo, core), seq: 16 (over y, z_hi), tile: 4 (over x).
Axes of the slice: x: 4, y: 4, z: 8 (z_hi: 4, z_lo: 2; z = z_hi * 2 + z_lo), core: 2. Of those that a mesh axis runs over, the one named last changes fastest.
Arguments:
- base_q: bfloat16 [4, 32, 32, 3072], P('grp', 'seq', None, 'tile'), may hold values from -20 to 20
- base_k: bfloat16 [4, 32, 32, 3072], P('grp', 'seq', None, 'tile'), may hold values from -20 to 20
- base_v: bfloat16 [4, 32, 32, 3072], P('grp', 'seq', None, 'tile'), may hold values from -6 to 6
- frame_stretch: int32 [4], replicated, may hold values from 0 to 1, never falling along the last dimension, each value on 1 to 3 neighbouring positions
- bridge_w: bfloat16 [3072, 1536], P('tile'), may hold values from -0.109375 to 0.109375
- sr_latent: bfloat16 [4, 64, 64, 1536], P(None, 'seq', 'tile'), may hold values from -6 to 6
- sr_wq: bfloat16 [1536, 1536], P(None, 'grp'), may hold values from -3 to 3
- sr_wk: bfloat16 [1536, 1536], P(None, 'grp'), may hold values from -3 to 3
- sr_wv: bfloat16 [1536, 1536], P(None, 'grp'), may hold values from -0.15625 to 0.15625
Outputs:
- sr_out: bfloat16 [4, 64, 64, 1536], P(None, 'seq', 'tile', 'grp')
The draws below stay inside these ranges and needn't reach their ends.
All inputs are finite; a program needn't handle non-finite values.
Results may differ from the reference program's by a relative error of at most 0.033.
Values may be sent and summed in bfloat16 or wider, within the bound.
A program may use at most 128 MiB of HBM per device.

```python
import math
import jax
import jax.numpy as jnp
import numpy as np
from jax import lax

HEAD = 128
HEADS_BASE = 24
HEADS_SR = 12
RAD = 2
STRETCH_MOST = 3
WB = 32
D_BASE = 3072
D_SR = 1536
FRAMES = 4
HB = 32
HS = 64
WS = 64
STRETCHES = 2


def draw_base_q(key, part):
    key = jax.random.fold_in(key, 1)
    shape = (FRAMES, HB, WB, D_BASE)
    return jnp.clip(jax.random.normal(key, shape, jnp.float32), -6.0, 6.0).astype(jnp.bfloat16)


def draw_base_k(key, part):
    key = jax.random.fold_in(key, 2)
    shape = (FRAMES, HB, WB, D_BASE)
    return jnp.clip(jax.random.normal(key, shape, jnp.float32), -6.0, 6.0).astype(jnp.bfloat16)


def draw_sr_wq(key, part):
    key = jax.random.fold_in(key, 3)
    scale = 1.0 / jnp.sqrt(jnp.float32(D_SR))
    return (jnp.clip(jax.random.normal(key, (D_SR, D_SR), jnp.float32), -6.0, 6.0) * scale).astype(jnp.bfloat16)


def draw_sr_wk(key, part):
    key = jax.random.fold_in(key, 4)
    scale = 1.0 / jnp.sqrt(jnp.float32(D_SR))
    return (jnp.clip(jax.random.normal(key, (D_SR, D_SR), jnp.float32), -6.0, 6.0) * scale).astype(jnp.bfloat16)


def steps_of(own_key, dims, pieces, smallest, largest):
    level, own = 1.0, jax.random.fold_in(own_key, 6)
    for dim, shards_of in pieces:
        heights = jnp.exp(jax.random.uniform(jax.random.fold_in(own, dim), (shards_of,), jnp.float32, smallest / len(pieces), largest / len(pieces)))
        level = level * jnp.repeat(heights, dims[dim] // shards_of).reshape([-1 if axis == dim else 1 for axis in range(len(dims))])
    return level


def split_up(count, total, bound, slope):
    portions = [(1 << 20) // math.isqrt(standing ** slope) + 1 for standing in range(2, count + 1)]
    rest, holding = total - bound - (count - 1), [1] * (count - 1)
    while rest > 0:
        free = [i for i in range(count - 1) if holding[i] < bound]
        mass, remaining = sum([portions[i] for i in free]), rest
        for i in free:
            extra = min(bound - holding[i], max(1, remaining * portions[i] // mass), rest)
            holding[i] = holding[i] + extra
            rest = rest - extra
    return np.array([bound] + holding)


def uneven(own_key, amount, total, reach, skew):
    if amount == 2:
        one = jax.random.randint(own_key, (), max(1, total - reach), min(reach, total - 1) + 1)
        return jnp.stack([one, total - one])
    tallies = jnp.asarray(split_up(amount, total, reach, skew), jnp.int32)
    twos = (amount - 1) // 2
    source_of, receiver = tallies[1:1 + 2 * twos:2], tallies[2:2 + 2 * twos:2]
    slack = jnp.minimum(source_of - 1, reach - receiver)
    moved = jax.random.randint(jax.random.fold_in(own_key, 1), (twos,), 0, 1 << 20) % (slack + 1)
    tallies = tallies.at[1:1 + 2 * twos:2].set(source_of - moved).at[2:2 + 2 * twos:2].set(receiver + moved)
    return tallies[jax.random.permutation(jax.random.fold_in(own_key, 2), amount)]


def normal_values(rng, extent, spread, most, split=(), kind=jnp.bfloat16):
    level = steps_of(rng, extent, split, -0.22, 0.18) if split else 1.0
    result = jax.random.normal(rng, extent, jnp.float32) * spread * level
    return jnp.minimum(jnp.maximum(result, -most), most).astype(kind)


def setup_inputs(seed: int = 0) -> dict:
    keys = jax.random.split(jax.random.key(seed), 10)
    base_q = draw_base_q(jax.random.fold_in(keys[9], 71), 0)
    base_k = draw_base_k(jax.random.fold_in(keys[9], 71), 0)
    base_v = normal_values(keys[2], (FRAMES, HB, WB, D_BASE), 1.0, 6.0, ((0, 4), (1, 16), (3, 4)))
    frame_stretch = jnp.searchsorted(jnp.cumsum(uneven(keys[3], STRETCHES, FRAMES, STRETCH_MOST, 0)), jnp.arange(FRAMES), side="right").astype(jnp.int32)
    bridge_w = normal_values(keys[4], (D_BASE, D_SR), D_BASE ** -0.5, 0.109375, ((0, 4),))
    sr_latent = normal_values(keys[5], (FRAMES, HS, WS, D_SR), 1.0, 6.0, ((1, 16), (2, 4)))
    sr_wq = draw_sr_wq(jax.random.fold_in(keys[9], 71), 0)
    sr_wk = draw_sr_wk(jax.random.fold_in(keys[9], 71), 0)
    sr_wv = normal_values(keys[8], (D_SR, D_SR), D_SR ** -0.5, 0.15625, ((1, 4),))
    return {"base_q": base_q, "base_k": base_k, "base_v": base_v, "frame_stretch": frame_stretch, "bridge_w": bridge_w, "sr_latent": sr_latent, "sr_wq": sr_wq, "sr_wk": sr_wk, "sr_wv": sr_wv}


def stretch_lookup(frame_ids, frame_stretch):
    matches = frame_ids[:, None] == jnp.arange(frame_stretch.shape[0], dtype=jnp.int32)[None, :]
    return lax.optimization_barrier(jnp.sum(jnp.where(matches, frame_stretch[None, :], 0), axis=1)).astype(jnp.int32)

def reference(base_q, base_k, base_v, frame_stretch, bridge_w, sr_latent, sr_wq, sr_wk, sr_wv):
    score_scale = HEAD ** (-0.5)
    tokens = FRAMES * HB * WB
    token_frame = (jnp.arange(tokens, dtype=jnp.int32) // (HB * WB)).astype(jnp.int32)
    token_stretch = stretch_lookup(token_frame, frame_stretch)
    block_rows = math.gcd(tokens, 1024)

    def by_head(array):
        return array.reshape(tokens, HEADS_BASE, HEAD).transpose(1, 0, 2)

    def base_head(operands):
        head_q, head_k, head_v = operands

        def query_block(number):
            first_row = (number * block_rows).astype(jnp.int32)
            rows_q = lax.dynamic_slice_in_dim(head_q, first_row, block_rows, 0)
            rows_stretch = lax.dynamic_slice_in_dim(token_stretch, first_row, block_rows, 0)
            scores = jnp.dot(rows_q, head_k.T, preferred_element_type=jnp.float32) * score_scale
            visible = token_stretch[None, :] <= rows_stretch[:, None]
            row_top = lax.optimization_barrier(jnp.max(jnp.where(visible, scores, -jnp.inf), axis=1, keepdims=True))
            unscaled = jnp.where(visible, jnp.exp(scores - row_top), 0.0)
            row_total = lax.optimization_barrier(jnp.sum(unscaled, axis=1, keepdims=True))
            blended = jnp.dot(unscaled.astype(jnp.bfloat16), head_v, preferred_element_type=jnp.float32) / row_total
            return blended.astype(jnp.bfloat16)
        return lax.map(query_block, jnp.arange(tokens // block_rows, dtype=jnp.int32)).reshape(tokens, HEAD)
    attended = lax.map(base_head, (by_head(base_q), by_head(base_k), by_head(base_v)))
    attended = attended.transpose(1, 0, 2).reshape(tokens, HEADS_BASE * HEAD)
    condition = jnp.dot(attended, bridge_w, preferred_element_type=jnp.float32).reshape(FRAMES, HB, WB, D_SR)
    condition = condition * lax.rsqrt(lax.optimization_barrier(jnp.mean(condition * condition, axis=-1, keepdims=True)) + 1e-06)
    upsampled = jnp.repeat(jnp.repeat(condition, 2, axis=1), 2, axis=2)
    hidden = sr_latent.astype(jnp.float32) + upsampled
    normed = (hidden * lax.rsqrt(lax.optimization_barrier(jnp.mean(hidden * hidden, axis=-1, keepdims=True)) + 1e-06)).astype(jnp.bfloat16)
    flat_cells = normed.reshape(-1, D_SR)

    def sr_project(weight):
        product = jnp.dot(flat_cells, weight, preferred_element_type=jnp.float32).astype(jnp.bfloat16)
        return product.reshape(FRAMES, HS, WS, HEADS_SR, HEAD).transpose(3, 0, 1, 2, 4)
    inside = jnp.pad(jnp.ones((HS, WS), dtype=bool), RAD)
    span = 2 * RAD + 1

    def sr_head(operands):
        head_q, head_k, head_v = operands
        query_wide = head_q.astype(jnp.float32)
        padding = ((0, 0), (RAD, RAD), (RAD, RAD), (0, 0))
        keys_pad = jnp.pad(head_k, padding)
        values_pad = jnp.pad(head_v, padding)
        score_list = []
        mask_list = []
        for row_step in range(span):
            for col_step in range(span):
                shifted = keys_pad[:, row_step:row_step + HS, col_step:col_step + WS].astype(jnp.float32)
                score_list.append(lax.optimization_barrier(jnp.sum(query_wide * shifted, axis=-1)) * score_scale)
                window = inside[row_step:row_step + HS, col_step:col_step + WS]
                mask_list.append(jnp.broadcast_to(window[None], (FRAMES, HS, WS)))
        scores = jnp.stack(score_list)
        allowed = jnp.stack(mask_list)
        row_top = lax.optimization_barrier(jnp.max(jnp.where(allowed, scores, -jnp.inf), axis=0))
        unscaled = jnp.where(allowed, jnp.exp(scores - row_top), 0.0)
        weights = (unscaled / lax.optimization_barrier(jnp.sum(unscaled, axis=0))).astype(jnp.bfloat16)
        blended = jnp.zeros(head_q.shape, jnp.float32)
        for row_step in range(span):
            for col_step in range(span):
                position = row_step * span + col_step
                shifted = values_pad[:, row_step:row_step + HS, col_step:col_step + WS].astype(jnp.float32)
                blended = blended + weights[position].astype(jnp.float32)[..., None] * shifted
        return blended.astype(jnp.bfloat16)
    heads_out = lax.map(sr_head, (sr_project(sr_wq), sr_project(sr_wk), sr_project(sr_wv)))
    return heads_out.transpose(1, 2, 3, 0, 4).reshape(FRAMES, HS, WS, D_SR)
```

```python
import functools
import math

import jax
import jax.numpy as jnp
from jax import lax
from jax.experimental import pallas as pl
from jax.experimental.pallas import tpu as pltpu
from jax.sharding import PartitionSpec as P

HEAD = 128
HEADS_TILE = 6
EPS = 1e-06
LOW = -1e30
EXP2_SCALE = HEAD ** (-0.5) * math.log2(math.e)
MESH = pl.DeviceIdType.MESH
BF16 = jnp.bfloat16
F32 = jnp.float32
NT = (((1,), (1,)), ((), ()))


def iota(shape, dim):
    return lax.broadcasted_iota(jnp.int32, shape, dim)


def one_hot(mask):
    return jnp.where(mask, 1.0, 0.0).astype(BF16)


def dot(a, b):
    return jnp.dot(a, b, preferred_element_type=F32)


def kernel(
    q_hbm, k_hbm, v_hbm, stretch, wb_hbm, lat_hbm, wq_hbm, wk_hbm, wv_hbm, out_hbm,
    q_buf, k_buf, v_buf, m_ref, l_ref, acc_ref, o_buf, a_buf, wb, wq, wk, wv,
    lat, edge_out, edge_in, p_own, p_send, p_recv, cond, x_buf, sr_q, sr_k, sr_v, out_buf,
    first_send, first_recv, own_send, fwd_send, relay_send, second_recv, ret_send, ret_recv,
    tile_send, tile_recv, cond_send, cond_recv, row_send, row_recv, col_send, col_recv,
    load_sem, out_sem,
):
    g, s, t = (lax.axis_index(name) for name in ("grp", "seq", "tile"))
    zl, c = g // 2, g % 2
    y, zh = s // 4, s % 4
    z = zh * 2 + zl
    sib = zl * 2 + (1 - c)
    s_up, s_down = (s + 1) % 16, (s + 15) % 16

    def dev(grp, seq, tile=t):
        return {"grp": grp, "seq": seq, "tile": tile}

    def remote(src, dst, send, recv, to):
        return pltpu.make_async_remote_copy(
            src_ref=src, dst_ref=dst, send_sem=send, recv_sem=recv, device_id=to, device_id_type=MESH
        )

    def landed(ref, sem):
        pltpu.make_async_copy(ref, ref, sem).wait()

    partners = [dev(((z + i) % 8) % 2 * 2 + c, y * 4 + ((z + i) % 8) // 2) for i in range(1, 8)]
    partners += [dev(g, (y + 1) % 4 * 4 + zh), dev(g, (y + 3) % 4 * 4 + zh), dev(sib, s)]
    partners += [dev(g, s, (t + i) % 4) for i in range(1, 4)]
    partners += [dev(i * 2 + c, other) for i in range(2) for other in (s_up, s_down)]
    barrier = pltpu.get_barrier_semaphore()
    for partner in partners:
        pl.semaphore_signal(barrier, inc=1, device_id=partner, device_id_type=MESH)
    pl.semaphore_wait(barrier, len(partners))

    first = ((k_hbm, k_buf.at[g, s]), (q_hbm, q_buf.at[zl, zh]), (v_hbm, v_buf.at[g, s]))

    def first_copy(i, h):
        src = first[i][0].at[:, h * HEAD:(h + 1) * HEAD]
        return remote(
            src, first[i][1], first_send.at[i, h], first_recv.at[i, zl, zh],
            dev(h % 2 * 2 + c, y * 4 + h // 2),
        )

    for i in range(3):
        for h in range(HEADS_TILE):
            @pl.when(z != h)
            def _():
                first_copy(i, h).start()

            @pl.when(z == h)
            def _():
                pltpu.make_async_copy(
                    first[i][0].at[:, h * HEAD:(h + 1) * HEAD], first[i][1], first_recv.at[i, zl, zh]
                ).start()

    loads = [
        pltpu.make_async_copy(src, dst, load_sem.at[i])
        for i, (src, dst) in enumerate(
            ((wb_hbm, wb), (lat_hbm, lat.at[:, 2:6]), (wq_hbm, wq), (wk_hbm, wk), (wv_hbm, wv))
        )
    ]
    for load in loads:
        load.start()
    mine, theirs = pl.ds(2 * c, 2), pl.ds(2 * (1 - c), 2)
    row_copies = [
        remote(lat_hbm.at[mine, 2:4], lat.at[mine, 0:2], row_send.at[0], row_recv.at[0], dev(g, s_up)),
        remote(lat_hbm.at[mine, 0:2], lat.at[mine, 6:8], row_send.at[1], row_recv.at[1], dev(g, s_down)),
    ]
    for copy in row_copies:
        copy.start()

    y_up, y_down, y_far = (y + 1) % 4, (y + 3) % 4, (y + 2) % 4
    bufs = (k_buf, v_buf)

    def region(kind, frame, row):
        return bufs[kind].at[frame, pl.ds(4 * row, 4)]

    def second(kind, frame, row, send, to):
        ref = region(kind, frame, row)
        return remote(ref, ref, send, second_recv.at[kind, frame, row], to)

    def attend(row, core):
        def half(i, carry):
            own = stretch[2 * i + c]
            queries = q_buf[i].reshape(256, HEAD)
            scores, lows = [], []
            for part in range(2):
                frame = 2 * part + core
                keys = k_buf[frame, pl.ds(4 * row, 4)].reshape(256, HEAD)
                scores.append(lax.dot_general(queries, keys, NT, preferred_element_type=F32))
                lows.append(jnp.where(stretch[frame] <= own, 0.0, LOW))
            top = m_ref[i]
            block_top = jnp.maximum(
                jnp.max(scores[0], axis=1, keepdims=True) + lows[0],
                jnp.max(scores[1], axis=1, keepdims=True) + lows[1],
            )
            new_top = jnp.maximum(top, block_top)
            carried = jnp.exp2((top - new_top) * EXP2_SCALE)
            shift = new_top[:, :1] * EXP2_SCALE
            total = l_ref[i] * carried
            blended = acc_ref[i] * carried
            for part in range(2):
                frame = 2 * part + core
                weights = jnp.exp2(scores[part] * EXP2_SCALE - (shift - lows[part]))
                total += weights[:, :HEAD] + weights[:, HEAD:]
                values = v_buf[frame, pl.ds(4 * row, 4)].reshape(256, HEAD)
                blended += dot(weights.astype(BF16), values)
            m_ref[i] = new_top
            l_ref[i] = total
            acc_ref[i] = blended
            return carry

        lax.fori_loop(0, 2, half, 0)

    @pl.when(z < HEADS_TILE)
    def _():
        m_ref[...] = jnp.full_like(m_ref, LOW)
        l_ref[...] = jnp.zeros_like(l_ref)
        acc_ref[...] = jnp.zeros_like(acc_ref)
        pending = []

        def send(copy):
            copy.start()
            pending.append(copy)

        for kind in range(2):
            for i in range(2):
                frame = 2 * i + c
                for j in range(4):
                    landed(bufs[kind].at[frame, 4 * y + j], first_recv.at[2 * kind, i, j])
                send(second(kind, frame, y, own_send.at[kind, i, 0], dev(g, y_up * 4 + zh)))
                send(second(kind, frame, y, own_send.at[kind, i, 1], dev(g, y_down * 4 + zh)))
                send(second(kind, frame, y, own_send.at[kind, i, 2], dev(sib, s)))
            if kind == 0:
                for i in range(2):
                    for j in range(4):
                        landed(q_buf.at[i, j], first_recv.at[1, i, j])

        for step, row in enumerate((y, y_down, y_up, y_far)):
            if step > 0:
                for kind in range(2):
                    for i in range(2):
                        frame = 2 * i + c
                        landed(region(kind, frame, row), second_recv.at[kind, frame, row])
                        if (step, kind) == (1, 0):
                            send(second(kind, frame, row, fwd_send.at[kind, i], dev(g, y_up * 4 + zh)))
                        if (step, kind) == (2, 1):
                            send(second(kind, frame, row, fwd_send.at[kind, i], dev(g, y_down * 4 + zh)))
                        send(second(kind, frame, row, relay_send.at[step - 1, kind, i], dev(sib, s)))
            attend(row, c)
            for kind in range(2):
                for i in range(2):
                    frame = 2 * i + 1 - c
                    landed(region(kind, frame, row), second_recv.at[kind, frame, row])
            attend(row, 1 - c)

        for i in range(2):
            total = jnp.sum(l_ref[i], axis=1, keepdims=True)
            o_buf[i] = (acc_ref[i] / total).astype(BF16).reshape(4, 64, HEAD)

        columns = pl.ds(pl.multiple_of(z * HEAD, HEAD), HEAD)

        def returned(i, j):
            return remote(
                o_buf.at[i, j], a_buf.at[:, columns], ret_send.at[i, j], ret_recv.at[z],
                dev(2 * i + c, y * 4 + j),
            )

        for i in range(2):
            for j in range(4):
                @pl.when(z != 2 * j + i)
                def _():
                    returned(i, j).start()

                @pl.when(z == 2 * j + i)
                def _():
                    pltpu.make_async_copy(o_buf.at[i, j], a_buf.at[:, columns], ret_recv.at[z]).start()
        for copy in pending:
            copy.wait_send()
        for i in range(2):
            for j in range(4):
                @pl.when(z != 2 * j + i)
                def _():
                    returned(i, j).wait_send()

    row_relays = []
    for i, rows in enumerate((slice(0, 2), slice(6, 8))):
        landed(lat.at[mine, rows], row_recv.at[i])
        ref = lat.at[mine, rows]
        row_relays.append(remote(ref, ref, row_send.at[2 + i], row_recv.at[2 + i], dev(sib, s)))
        row_relays[-1].start()

    loads[0].wait()
    for h in range(HEADS_TILE):
        landed(a_buf.at[:, h * HEAD:(h + 1) * HEAD], ret_recv.at[h])
    attended = a_buf[...]
    row_id, token = iota((256, 64), 0), iota((256, 64), 1)
    partial = jnp.zeros((256, 512), F32)
    for part in range(3):
        place = (row_id & 31) - 10 * part
        column = (row_id >> 6) * 8 - 1 + place
        fits = (place >= 0) & (place < 10) & (column >= 0) & (column < 32)
        chosen = one_hot(fits & (((row_id >> 5) & 1) * 32 + column == token))
        rows = dot(chosen, attended).astype(BF16)
        partial += dot(rows, wb[:, 512 * part:512 * (part + 1)])
    p_own[...] = partial.reshape(4, 64, 512)
    p_send[...] = partial.astype(BF16).reshape(4, 64, 512)
    tile_copies = [
        remote(
            p_send.at[(t + i) % 4], p_recv.at[i - 1], tile_send.at[i - 1], tile_recv.at[i - 1],
            dev(g, s, (t + i) % 4),
        )
        for i in range(1, 4)
    ]
    for copy in tile_copies:
        copy.start()

    loads[1].wait()
    for i, rows in enumerate((slice(0, 2), slice(6, 8))):
        landed(lat.at[theirs, rows], row_recv.at[2 + i])
    flat_lat = lat[...].reshape(512, 1536)
    edge_id, cell = iota((64, 512), 0), iota((64, 512), 1)
    col_copies = []
    for i, (start, neighbour) in enumerate(((14, (t + 1) % 4), (0, (t + 3) % 4))):
        chosen = one_hot((edge_id >> 1) * 16 + (edge_id & 1) + start == cell)
        edge_out[i] = dot(chosen, flat_lat).astype(BF16)
        col_copies.append(
            remote(edge_out.at[i], edge_in.at[i], col_send.at[i], col_recv.at[i], dev(g, s, neighbour))
        )
        col_copies[-1].start()

    for i in range(3):
        landed(p_recv.at[i], tile_recv.at[i])
    summed = p_own[t]
    for i in range(3):
        summed += p_recv[i].astype(F32)
    squares = summed * summed
    squares = squares[:, :128] + squares[:, 128:256] + squares[:, 256:384] + squares[:, 384:]
    left, right = iota((64, 64), 0), iota((64, 64), 1)

    def token_of(row):
        place = row & 31
        return place - jnp.where(place >= 10, 10, 0) - jnp.where(place >= 20, 10, 0)

    same = ((left >> 5) == (right >> 5)) & (token_of(left) == token_of(right))
    together = jnp.dot(
        jnp.where(same, 1.0, 0.0), squares, preferred_element_type=F32, precision=lax.Precision.HIGHEST
    )
    mean = jnp.sum(together, axis=1, keepdims=True) * (1.0 / 1536)
    cond[g, 1:3] = (summed * lax.rsqrt(mean + EPS)).astype(BF16).reshape(2, 32, 512)

    slots = (slice(1, 3), slice(0, 1), slice(3, 4))

    def cond_copy(frame, src, slot, sem, to):
        return remote(cond.at[frame, src], cond.at[frame, slots[slot]], cond_send.at[sem], cond_recv.at[frame, slot], to)

    cond_copies = [
        cond_copy(g, slots[0], 0, 0, dev((1 - zl) * 2 + c, s)),
        cond_copy(g, slice(2, 3), 1, 1, dev(c, s_up)),
        cond_copy(g, slice(2, 3), 1, 2, dev(2 + c, s_up)),
        cond_copy(g, slice(1, 2), 2, 3, dev(c, s_down)),
        cond_copy(g, slice(1, 2), 2, 4, dev(2 + c, s_down)),
        cond_copy(g, slots[0], 0, 5, dev(sib, s)),
    ]
    for copy in cond_copies:
        copy.start()
    arrivals = [((1 - zl) * 2 + c, 0), (c, 1), (2 + c, 1), (c, 2), (2 + c, 2)]
    for i, (frame, slot) in enumerate(arrivals):
        landed(cond.at[frame, slots[slot]], cond_recv.at[frame, slot])
        cond_copies.append(cond_copy(frame, slots[slot], slot, 6 + i, dev(sib, s)))
        cond_copies[-1].start()
    for i in range(2):
        landed(edge_in.at[i], col_recv.at[i])
    for load in loads[2:]:
        load.wait()

    cell, source = iota((160, 128), 0), iota((160, 128), 1)
    side = cell - 128
    cell_row = jnp.where(cell < 128, cell >> 4, (side >> 1) & 7)
    cell_token = jnp.where(cell < 128, 1 + ((cell & 15) >> 1), jnp.where(side < 16, 0, 9))
    spread = [one_hot((cell_row >> 1) * 32 + 10 * part + cell_token == source) for part in range(3)]

    query, key = iota((64, 160), 0), iota((64, 160), 1)
    side = key - 128
    key_row = jnp.where(key < 128, key >> 4, (side >> 1) & 7)
    key_col = jnp.where(key < 128, 2 + (key & 15), (side & 1) + jnp.where(side < 16, 0, 18))
    row_off, col_off = key_row - (query >> 4) - 2, key_col - (query & 15) - 2
    row_at, col_at = 4 * s - 2 + key_row, 16 * t - 2 + key_col
    near = (jnp.abs(row_off) <= 2) & (jnp.abs(col_off) <= 2)
    near = near & (row_at >= 0) & (row_at < 64) & (col_at >= 0) & (col_at < 64)
    low = jnp.where(near, 0.0, LOW)

    def layer(core):
        def norm(i, carry):
            frame = 2 * i + core
            rows = pl.ds(pl.multiple_of(frame * 16, 16), 16)
            token_rows = cond[frame].reshape(128, 512)
            hidden, square = [], 0.0
            for part in range(3):
                lanes = slice(512 * part, 512 * (part + 1))
                cells = jnp.concatenate(
                    [lat[frame, :, :, lanes].reshape(128, 512), edge_in[0, rows, lanes], edge_in[1, rows, lanes]], axis=0
                ).astype(F32)
                cells = cells + dot(spread[part], token_rows)
                hidden.append(cells)
                square = square + jnp.sum(cells * cells, axis=1, keepdims=True)
            scale = lax.rsqrt(square * (1.0 / 1536) + EPS)
            for part in range(3):
                x_buf[i, :, 512 * part:512 * (part + 1)] = (hidden[part] * scale).astype(BF16)
            return carry

        lax.fori_loop(0, 2, norm, 0)
        cells = x_buf[...].reshape(320, 1536)
        sr_k[...] = dot(cells, wk[...]).astype(BF16).reshape(2, 160, 384)
        sr_v[...] = dot(cells, wv[...]).astype(BF16).reshape(2, 160, 384)
        sr_q[...] = dot(x_buf[:, 32:96].reshape(128, 1536), wq[...]).astype(BF16).reshape(2, 64, 384)

        def near_attention(i, carry):
            for h in range(3):
                lanes = slice(h * HEAD, (h + 1) * HEAD)
                scores = lax.dot_general(
                    sr_q[i, :, lanes], sr_k[i, :, lanes], NT, preferred_element_type=F32
                )
                scores = scores * HEAD ** (-0.5) + low
                unscaled = jnp.exp(scores - jnp.max(scores, axis=1, keepdims=True))
                weights = (unscaled / jnp.sum(unscaled, axis=1, keepdims=True)).astype(BF16)
                blended = dot(weights, sr_v[i, :, lanes]).astype(BF16)
                out_buf[2 * i + core, :, :, lanes] = blended.reshape(4, 16, HEAD)
            return carry

        lax.fori_loop(0, 2, near_attention, 0)

    layer(c)
    for frame, slot in [(sib, 0)] + [(2 * i + 1 - c, slot) for i, slot in ((0, 1), (1, 1), (0, 2), (1, 2))] + [((1 - zl) * 2 + 1 - c, 0)]:
        landed(cond.at[frame, slots[slot]], cond_recv.at[frame, slot])
    layer(1 - c)
    result = pltpu.make_async_copy(out_buf, out_hbm, out_sem)
    result.start()

    for i in range(3):
        for h in range(HEADS_TILE):
            @pl.when(z != h)
            def _():
                first_copy(i, h).wait_send()
    for copy in row_copies + row_relays + tile_copies + col_copies + cond_copies:
        copy.wait_send()
    result.wait()


def local(base_q, base_k, base_v, frame_stretch, bridge_w, sr_latent, sr_wq, sr_wk, sr_wv):
    hbm = pl.BlockSpec(memory_space=pl.ANY)
    dma = pltpu.SemaphoreType.DMA
    vmem = pltpu.VMEM
    call = pl.pallas_call(
        kernel,
        out_shape=jax.ShapeDtypeStruct((4, 4, 16, 384), BF16),
        in_specs=[hbm, hbm, hbm, pl.BlockSpec(memory_space=pltpu.SMEM)] + [hbm] * 5,
        out_specs=hbm,
        scratch_shapes=[
            vmem((2, 4, 64, HEAD), BF16),
            vmem((4, 16, 64, HEAD), BF16),
            vmem((4, 16, 64, HEAD), BF16),
            vmem((2, 256, HEAD), F32),
            vmem((2, 256, HEAD), F32),
            vmem((2, 256, HEAD), F32),
            vmem((2, 4, 64, HEAD), BF16),
            vmem((64, 768), BF16),
            vmem((768, 1536), BF16),
            vmem((1536, 384), BF16),
            vmem((1536, 384), BF16),
            vmem((1536, 384), BF16),
            vmem((4, 8, 16, 1536), BF16),
            vmem((2, 64, 1536), BF16),
            vmem((2, 64, 1536), BF16),
            vmem((4, 64, 512), F32),
            vmem((4, 64, 512), BF16),
            vmem((3, 64, 512), BF16),
            vmem((4, 4, 32, 512), BF16),
            vmem((2, 160, 1536), BF16),
            vmem((2, 64, 384), BF16),
            vmem((2, 160, 384), BF16),
            vmem((2, 160, 384), BF16),
            vmem((4, 4, 16, 384), BF16),
            dma((3, HEADS_TILE)),
            dma((3, 2, 4)),
            dma((2, 2, 3)),
            dma((2, 2)),
            dma((3, 2, 2)),
            dma((2, 4, 4)),
            dma((2, 4)),
            dma((HEADS_TILE,)),
            dma((3,)),
            dma((3,)),
            dma((11,)),
            dma((4, 3)),
            dma((4,)),
            dma((4,)),
            dma((2,)),
            dma((2,)),
            dma((5,)),
            dma,
        ],
        compiler_params=pltpu.CompilerParams(
            collective_id=0, has_side_effects=True, vmem_limit_bytes=50 * 1024 * 1024
        ),
        cost_estimate=pl.CostEstimate(flops=4 * 10**9, bytes_accessed=16 * 2**20, transcendentals=2 * 10**6),
    )
    return call(
        base_q.reshape(64, 768), base_k.reshape(64, 768), base_v.reshape(64, 768), frame_stretch,
        bridge_w, sr_latent, sr_wq, sr_wk, sr_wv,
    )


def solution(mesh):
    placed = (
        P("grp", "seq", None, "tile"),
        P("grp", "seq", None, "tile"),
        P("grp", "seq", None, "tile"),
        P(),
        P("tile", None),
        P(None, "seq", "tile", None),
        P(None, "grp"),
        P(None, "grp"),
        P(None, "grp"),
    )
    return jax.shard_map(
        local, mesh=mesh, in_specs=placed, out_specs=P(None, "seq", "tile", "grp"), check_vma=False
    )
```

```python
import functools
import math

import jax
import jax.numpy as jnp
from jax import lax
from jax.experimental import pallas as pl
from jax.experimental.pallas import tpu as pltpu
from jax.sharding import PartitionSpec as P

HEAD = 128
HEADS_TILE = 6
EPS = 1e-06
LOW = -1e30
EXP2_SCALE = HEAD ** (-0.5) * math.log2(math.e)
MESH = pl.DeviceIdType.MESH
BF16 = jnp.bfloat16
F32 = jnp.float32
NT = (((1,), (1,)), ((), ()))


def iota(shape, dim):
    return lax.broadcasted_iota(jnp.int32, shape, dim)


def one_hot(mask):
    return jnp.where(mask, 1.0, 0.0).astype(BF16)


def dot(a, b):
    return jnp.dot(a, b, preferred_element_type=F32)


def kernel(
    q_hbm, k_hbm, v_hbm, stretch_hbm, wb_hbm, lat_hbm, wq_hbm, wk_hbm, wv_hbm, out_hbm,
    stretch, q_buf, k_buf, v_buf, m_ref, l_ref, acc_ref, o_buf, a_buf, wb, wq, wk, wv,
    lat, lat_sq, lat_q, lat_k, lat_v, edge_out, p_own, p_send, p_recv, cond, tok, out_buf,
    first_send, first_recv, own_send, fwd_send, relay_send, second_recv, ret_send, ret_recv,
    tile_send, tile_recv, cond_send, cond_recv, row_send, row_recv, col_send, col_recv,
    load_sem, out_sem, near_sem,
):
    g, s, t = (lax.axis_index(name) for name in ("grp", "seq", "tile"))
    zl, c = g // 2, g % 2
    y, zh = s // 4, s % 4
    z = zh * 2 + zl
    sib = zl * 2 + (1 - c)
    s_up, s_down = (s + 1) % 16, (s + 15) % 16

    def dev(grp, seq, tile=t):
        return {"grp": grp, "seq": seq, "tile": tile}

    def remote(src, dst, send, recv, to):
        return pltpu.make_async_remote_copy(
            src_ref=src, dst_ref=dst, send_sem=send, recv_sem=recv, device_id=to, device_id_type=MESH
        )

    def landed(ref, sem):
        pltpu.make_async_copy(ref, ref, sem).wait()

    partners = [dev(((z + i) % 8) % 2 * 2 + c, y * 4 + ((z + i) % 8) // 2) for i in range(1, 8)]
    partners += [dev(g, (y + 1) % 4 * 4 + zh), dev(g, (y + 3) % 4 * 4 + zh), dev(sib, s)]
    partners += [dev(g, s, (t + i) % 4) for i in range(1, 4)]
    barrier = pltpu.get_barrier_semaphore()
    for partner in partners:
        pl.semaphore_signal(barrier, inc=1, device_id=partner, device_id_type=MESH)
    pl.semaphore_wait(barrier, len(partners))

    first = ((k_hbm, k_buf.at[g, s]), (v_hbm, v_buf.at[g, s]), (q_hbm, q_buf.at[zl, zh]))

    def first_copy(i, h):
        src = first[i][0].at[:, h * HEAD:(h + 1) * HEAD]
        return remote(
            src, first[i][1], first_send.at[i, h], first_recv.at[i, zl, zh],
            dev(h % 2 * 2 + c, y * 4 + h // 2),
        )

    for i in range(3):
        for h in range(HEADS_TILE):
            @pl.when(z != h)
            def _():
                first_copy(i, h).start()

            @pl.when(z == h)
            def _():
                pltpu.make_async_copy(
                    first[i][0].at[:, h * HEAD:(h + 1) * HEAD], first[i][1], first_recv.at[i, zl, zh]
                ).start()

    loads = [
        pltpu.make_async_copy(src, dst, load_sem.at[i])
        for i, (src, dst) in enumerate((
            (stretch_hbm, stretch), (lat_hbm, lat.at[:, 32:96]), (wk_hbm, wk), (wv_hbm, wv), (wq_hbm, wq), (wb_hbm, wb),
        ))
    ]
    for load in loads:
        load.start()

    y_up, y_down, y_far = (y + 1) % 4, (y + 3) % 4, (y + 2) % 4
    for other in (y_up, y_down):
        pl.semaphore_signal(near_sem, inc=1, device_id=dev(g, other * 4 + zh), device_id_type=MESH)
    pl.semaphore_wait(near_sem, 2)

    mine, theirs = pl.ds(2 * c, 2), pl.ds(2 * (1 - c), 2)
    row_copies = [
        remote(lat_hbm.at[mine, 32:64], lat.at[mine, 0:32], row_send.at[0], row_recv.at[0], dev(g, s_up)),
        remote(lat_hbm.at[mine, 0:32], lat.at[mine, 96:128], row_send.at[1], row_recv.at[1], dev(g, s_down)),
    ]
    for copy in row_copies:
        copy.start()

    def project(refs, rows):
        count = rows.stop - rows.start
        cells = lat[:, rows].reshape(4 * count, 1536)
        for weight, ref in refs:
            ref[:, rows] = dot(cells, weight[...]).reshape(4, count, 384)
        wide = cells.astype(F32)
        squares = wide[:, :HEAD] * wide[:, :HEAD]
        for i in range(1, 12):
            lanes = slice(HEAD * i, HEAD * (i + 1))
            squares += wide[:, lanes] * wide[:, lanes]
        lat_sq[:, rows] = squares.reshape(4, count, HEAD)

    for load in loads[:5]:
        load.wait()
    project(((wk, lat_k), (wv, lat_v)), slice(32, 96))
    lat_q[...] = dot(lat[:, 32:96].reshape(256, 1536), wq[...]).reshape(4, 64, 384)

    bufs = (k_buf, v_buf)

    def region(kind, frame, row):
        return bufs[kind].at[frame, pl.ds(4 * row, 4)]

    def second(kind, frame, row, send, to):
        ref = region(kind, frame, row)
        return remote(ref, ref, send, second_recv.at[kind, frame, row], to)

    def attend(row, core):
        def half(i, carry):
            own = stretch[2 * i + c]
            queries = q_buf[i].reshape(256, HEAD)
            scores, lows = [], []
            for part in range(2):
                frame = 2 * part + core
                keys = k_buf[frame, pl.ds(4 * row, 4)].reshape(256, HEAD)
                scores.append(lax.dot_general(queries, keys, NT, preferred_element_type=F32))
                lows.append(jnp.where(stretch[frame] <= own, 0.0, LOW))
            top = m_ref[i]
            block_top = jnp.maximum(
                jnp.max(scores[0], axis=1, keepdims=True) + lows[0],
                jnp.max(scores[1], axis=1, keepdims=True) + lows[1],
            )
            new_top = jnp.maximum(top, block_top)
            carried = jnp.exp2((top - new_top) * EXP2_SCALE)
            shift = new_top[:, :1] * EXP2_SCALE
            total = l_ref[i] * carried
            blended = acc_ref[i] * carried
            for part in range(2):
                frame = 2 * part + core
                weights = jnp.exp2(scores[part] * EXP2_SCALE - (shift - lows[part]))
                total += weights[:, :HEAD] + weights[:, HEAD:]
                values = v_buf[frame, pl.ds(4 * row, 4)].reshape(256, HEAD)
                blended += dot(weights.astype(BF16), values)
            m_ref[i] = new_top
            l_ref[i] = total
            acc_ref[i] = blended
            return carry

        for i in range(2):
            half(i, 0)

    @pl.when(z < HEADS_TILE)
    def _():
        m_ref[...] = jnp.full_like(m_ref, LOW)
        l_ref[...] = jnp.zeros_like(l_ref)
        acc_ref[...] = jnp.zeros_like(acc_ref)
        pending = []

        def send(copy):
            copy.start()
            pending.append(copy)

        for kind in range(2):
            for i in range(2):
                frame = 2 * i + c
                for j in range(4):
                    landed(bufs[kind].at[frame, 4 * y + j], first_recv.at[kind, i, j])
                send(second(kind, frame, y, own_send.at[kind, i, 0], dev(g, y_up * 4 + zh)))
                send(second(kind, frame, y, own_send.at[kind, i, 1], dev(g, y_down * 4 + zh)))
                send(second(kind, frame, y, own_send.at[kind, i, 2], dev(sib, s)))
        for i in range(2):
            for j in range(4):
                landed(q_buf.at[i, j], first_recv.at[2, i, j])

        def relay(step, row, kind):
            for i in range(2):
                frame = 2 * i + c
                landed(region(kind, frame, row), second_recv.at[kind, frame, row])
                if step == 0 and i == 0:
                    send(second(kind, frame, row, fwd_send.at[kind, i], dev(g, y_up * 4 + zh)))
                if step == 1 and i == 1:
                    send(second(kind, frame, row, fwd_send.at[kind, i], dev(g, y_down * 4 + zh)))
                send(second(kind, frame, row, relay_send.at[step, kind, i], dev(sib, s)))

        def from_sibling(row):
            for kind in range(2):
                for i in range(2):
                    frame = 2 * i + 1 - c
                    landed(region(kind, frame, row), second_recv.at[kind, frame, row])

        attend(y, c)
        relay(0, y_down, 0)
        relay(1, y_up, 0)
        from_sibling(y)
        attend(y, 1 - c)
        relay(0, y_down, 1)
        relay(1, y_up, 1)
        attend(y_down, c)
        attend(y_up, c)
        from_sibling(y_down)
        attend(y_down, 1 - c)
        relay(2, y_far, 0)
        from_sibling(y_up)
        attend(y_up, 1 - c)
        relay(2, y_far, 1)
        attend(y_far, c)
        from_sibling(y_far)
        attend(y_far, 1 - c)

        for i in range(2):
            total = jnp.sum(l_ref[i], axis=1, keepdims=True)
            o_buf[i] = (acc_ref[i] / total).astype(BF16).reshape(4, 64, HEAD)

        def returned(i, j):
            return remote(
                o_buf.at[i, j], a_buf.at[z], ret_send.at[i, j], ret_recv.at[z],
                dev(2 * i + c, y * 4 + j),
            )

        for i in range(2):
            for j in range(4):
                @pl.when(z != 2 * j + i)
                def _():
                    returned(i, j).start()

                @pl.when(z == 2 * j + i)
                def _():
                    pltpu.make_async_copy(o_buf.at[i, j], a_buf.at[z], ret_recv.at[z]).start()
        for copy in pending:
            copy.wait_send()
        for i in range(2):
            for j in range(4):
                @pl.when(z != 2 * j + i)
                def _():
                    returned(i, j).wait_send()

    row_relays = []
    for i, rows in enumerate((slice(0, 32), slice(96, 128))):
        landed(lat.at[mine, rows], row_recv.at[i])
        ref = lat.at[mine, rows]
        row_relays.append(remote(ref, ref, row_send.at[2 + i], row_recv.at[2 + i], dev(sib, s)))
        row_relays[-1].start()

    loads[5].wait()
    for h in range(HEADS_TILE):
        landed(a_buf.at[h], ret_recv.at[h])
    attended = jnp.concatenate([a_buf[h] for h in range(HEADS_TILE)], axis=1)
    row_id, token = iota((256, 64), 0), iota((256, 64), 1)
    partial = jnp.zeros((256, 512), F32)
    for part in range(3):
        place = (row_id & 31) - 10 * part
        column = (row_id >> 6) * 8 - 1 + place
        fits = (place >= 0) & (place < 10) & (column >= 0) & (column < 32)
        chosen = one_hot(fits & (((row_id >> 5) & 1) * 32 + column == token))
        rows = dot(chosen, attended).astype(BF16)
        partial += dot(rows, wb[:, 512 * part:512 * (part + 1)])
    p_own[...] = partial.reshape(4, 64, 512)
    p_send[...] = partial.astype(BF16).reshape(4, 64, 512)
    tile_copies = [
        remote(
            p_send.at[(t + i) % 4], p_recv.at[i - 1], tile_send.at[i - 1], tile_recv.at[i - 1],
            dev(g, s, (t + i) % 4),
        )
        for i in range(1, 4)
    ]
    for copy in tile_copies:
        copy.start()

    for i, rows in enumerate((slice(0, 32), slice(96, 128))):
        landed(lat.at[theirs, rows], row_recv.at[2 + i])
    edge_id, cell = iota((32, 128), 0), iota((32, 128), 1)
    edge_cell = ((edge_id >> 1) & 7) * 16 + (edge_id & 1) + jnp.where(edge_id < 16, 14, 0)
    chosen = one_hot(edge_cell == cell)
    for frame in range(4):
        edges = dot(chosen, lat[frame, 0:128]).astype(BF16)
        edge_out[0, frame], edge_out[1, frame] = edges[:16], edges[16:]
    sides = (slice(128, 144), slice(144, 160))
    col_copies = [
        remote(edge_out.at[i], lat.at[:, sides[i]], col_send.at[i], col_recv.at[i], dev(g, s, neighbour))
        for i, neighbour in enumerate(((t + 1) % 4, (t + 3) % 4))
    ]
    for copy in col_copies:
        copy.start()
    for rows in (slice(0, 32), slice(96, 128)):
        project(((wk, lat_k), (wv, lat_v)), rows)

    for i in range(3):
        landed(p_recv.at[i], tile_recv.at[i])
    summed = p_own[t]
    for i in range(3):
        summed += p_recv[i].astype(F32)
    squares = summed * summed
    squares = squares[:, :128] + squares[:, 128:256] + squares[:, 256:384] + squares[:, 384:]
    left, right = iota((64, 64), 0), iota((64, 64), 1)

    def token_of(row):
        place = row & 31
        return place - jnp.where(place >= 10, 10, 0) - jnp.where(place >= 20, 10, 0)

    same = ((left >> 5) == (right >> 5)) & (token_of(left) == token_of(right))
    together = jnp.dot(
        jnp.where(same, 1.0, 0.0), squares, preferred_element_type=F32, precision=lax.Precision.HIGHEST
    )
    mean = jnp.sum(together, axis=1, keepdims=True) * (1.0 / 1536)
    cond[g, 1:3] = (summed * lax.rsqrt(mean + EPS)).astype(BF16).reshape(2, 32, 512)

    slots = (slice(1, 3), slice(0, 1), slice(3, 4))

    def cond_copy(frame, src, slot, sem, to):
        return remote(cond.at[frame, src], cond.at[frame, slots[slot]], cond_send.at[sem], cond_recv.at[frame, slot], to)

    cond_copies = [
        cond_copy(g, slots[0], 0, 0, dev((1 - zl) * 2 + c, s)),
        cond_copy(g, slice(2, 3), 1, 1, dev(c, s_up)),
        cond_copy(g, slice(2, 3), 1, 2, dev(2 + c, s_up)),
        cond_copy(g, slice(1, 2), 2, 3, dev(c, s_down)),
        cond_copy(g, slice(1, 2), 2, 4, dev(2 + c, s_down)),
        cond_copy(g, slots[0], 0, 5, dev(sib, s)),
    ]
    for copy in cond_copies:
        copy.start()
    for i in range(2):
        landed(lat.at[:, sides[i]], col_recv.at[i])
    project(((wk, lat_k), (wv, lat_v)), slice(128, 160))
    arrivals = [((1 - zl) * 2 + c, 0), (c, 1), (2 + c, 1), (c, 2), (2 + c, 2)]
    for i, (frame, slot) in enumerate(arrivals):
        landed(cond.at[frame, slots[slot]], cond_recv.at[frame, slot])
        cond_copies.append(cond_copy(frame, slots[slot], slot, 6 + i, dev(sib, s)))
        cond_copies[-1].start()

    place, source = iota((64, 128), 0), iota((64, 128), 1)
    unpack = [
        one_hot(((place & 15) < 10) & ((place >> 4) * 32 + 10 * part + (place & 15) == source)) for part in range(3)
    ]
    cell, source = iota((160, 64), 0), iota((160, 64), 1)
    side = cell - 128
    cell_row = jnp.where(cell < 128, cell >> 4, (side >> 1) & 7)
    cell_token = jnp.where(cell < 128, 1 + ((cell & 15) >> 1), jnp.where(side < 16, 0, 9))
    above = (cell_row >> 1) * 16 + cell_token == source
    spread = one_hot(above)
    diagonal = iota((64, 64), 0) == iota((64, 64), 1)

    query, key = iota((64, 160), 0), iota((64, 160), 1)
    side = key - 128
    key_row = jnp.where(key < 128, key >> 4, (side >> 1) & 7)
    key_col = jnp.where(key < 128, 2 + (key & 15), (side & 1) + jnp.where(side < 16, 0, 18))
    row_off, col_off = key_row - (query >> 4) - 2, key_col - (query & 15) - 2
    row_at, col_at = 4 * s - 2 + key_row, 16 * t - 2 + key_col
    near = (jnp.abs(row_off) <= 2) & (jnp.abs(col_off) <= 2)
    near = near & (row_at >= 0) & (row_at < 64) & (col_at >= 0) & (col_at < 64)
    low = jnp.where(near, 0.0, LOW)

    def layer(core):
        for i in range(2):
            rows = cond[2 * i + core].reshape(128, 512)
            for part in range(3):
                tok[i, :, 512 * part:512 * (part + 1)] = dot(unpack[part], rows).astype(BF16)
        tokens = tok[...].reshape(128, 1536)
        parts = [dot(tokens, weight[...]).astype(BF16) for weight in (wk, wv, wq)]
        for i in range(2):
            frame = 2 * i + core
            pair = lax.dot_general(tok[i], tok[i], NT, preferred_element_type=F32)
            token_sq = jnp.sum(jnp.where(diagonal, pair, 0.0), axis=0, keepdims=True)
            cross = lax.dot_general(lat[frame], tok[i], NT, preferred_element_type=F32)
            square = jnp.sum(jnp.where(above, 2.0 * cross + token_sq, 0.0), axis=1, keepdims=True)
            square = jnp.maximum(square + jnp.sum(lat_sq[frame], axis=1, keepdims=True), 0.0)
            scale = lax.rsqrt(square * (1.0 / 1536) + EPS)
            keys, values = (
                (scale * (ref[frame] + dot(spread, part[64 * i:64 * (i + 1)]))).astype(BF16)
                for ref, part in ((lat_k, parts[0]), (lat_v, parts[1]))
            )
            queries = dot(spread[32:96], parts[2][64 * i:64 * (i + 1)])
            queries = (scale[32:96] * (lat_q[frame] + queries)).astype(BF16)
            for h in range(3):
                lanes = slice(h * HEAD, (h + 1) * HEAD)
                scores = lax.dot_general(queries[:, lanes], keys[:, lanes], NT, preferred_element_type=F32)
                scores = scores * HEAD ** (-0.5) + low
                unscaled = jnp.exp(scores - jnp.max(scores, axis=1, keepdims=True))
                weights = (unscaled / jnp.sum(unscaled, axis=1, keepdims=True)).astype(BF16)
                blended = dot(weights, values[:, lanes]).astype(BF16)
                out_buf[frame, :, :, lanes] = blended.reshape(4, 16, HEAD)

    layer(c)
    for frame, slot in [(sib, 0)] + [(2 * i + 1 - c, slot) for i, slot in ((0, 1), (1, 1), (0, 2), (1, 2))] + [((1 - zl) * 2 + 1 - c, 0)]:
        landed(cond.at[frame, slots[slot]], cond_recv.at[frame, slot])
    layer(1 - c)
    result = pltpu.make_async_copy(out_buf, out_hbm, out_sem)
    result.start()

    for i in range(3):
        for h in range(HEADS_TILE):
            @pl.when(z != h)
            def _():
                first_copy(i, h).wait_send()
    for copy in row_copies + row_relays + tile_copies + col_copies + cond_copies:
        copy.wait_send()
    result.wait()


def local(base_q, base_k, base_v, frame_stretch, bridge_w, sr_latent, sr_wq, sr_wk, sr_wv):
    hbm = pl.BlockSpec(memory_space=pltpu.HBM)
    dma = pltpu.SemaphoreType.DMA
    vmem = pltpu.VMEM
    call = pl.pallas_call(
        kernel,
        out_shape=jax.ShapeDtypeStruct((4, 4, 16, 384), BF16),
        in_specs=[hbm] * 9,
        out_specs=hbm,
        scratch_shapes=[
            pltpu.SMEM((4,), jnp.int32),
            vmem((2, 4, 64, HEAD), BF16),
            vmem((4, 16, 64, HEAD), BF16),
            vmem((4, 16, 64, HEAD), BF16),
            vmem((2, 256, HEAD), F32),
            vmem((2, 256, HEAD), F32),
            vmem((2, 256, HEAD), F32),
            vmem((2, 4, 64, HEAD), BF16),
            vmem((HEADS_TILE, 64, HEAD), BF16),
            vmem((768, 1536), BF16),
            vmem((1536, 384), BF16),
            vmem((1536, 384), BF16),
            vmem((1536, 384), BF16),
            vmem((4, 160, 1536), BF16),
            vmem((4, 160, HEAD), F32),
            vmem((4, 64, 384), F32),
            vmem((4, 160, 384), F32),
            vmem((4, 160, 384), F32),
            vmem((2, 4, 16, 1536), BF16),
            vmem((4, 64, 512), F32),
            vmem((4, 64, 512), BF16),
            vmem((3, 64, 512), BF16),
            vmem((4, 4, 32, 512), BF16),
            vmem((2, 64, 1536), BF16),
            vmem((4, 4, 16, 384), BF16),
            dma((3, HEADS_TILE)),
            dma((3, 2, 4)),
            dma((2, 2, 3)),
            dma((2, 2)),
            dma((3, 2, 2)),
            dma((2, 4, 4)),
            dma((2, 4)),
            dma((HEADS_TILE,)),
            dma((3,)),
            dma((3,)),
            dma((11,)),
            dma((4, 3)),
            dma((4,)),
            dma((4,)),
            dma((2,)),
            dma((2,)),
            dma((6,)),
            dma,
            pltpu.SemaphoreType.REGULAR,
        ],
        compiler_params=pltpu.CompilerParams(
            collective_id=0, has_side_effects=True, vmem_limit_bytes=62 * 1024 * 1024
        ),
        cost_estimate=pl.CostEstimate(flops=4 * 10**9, bytes_accessed=16 * 2**20, transcendentals=2 * 10**6),
    )
    return call(
        base_q.reshape(64, 768), base_k.reshape(64, 768), base_v.reshape(64, 768), frame_stretch,
        bridge_w, sr_latent.reshape(4, 64, 1536), sr_wq, sr_wk, sr_wv,
    )


def solution(mesh):
    placed = (
        P("grp", "seq", None, "tile"),
        P("grp", "seq", None, "tile"),
        P("grp", "seq", None, "tile"),
        P(),
        P("tile", None),
        P(None, "seq", "tile", None),
        P(None, "grp"),
        P(None, "grp"),
        P(None, "grp"),
    )
    return jax.shard_map(
        local, mesh=mesh, in_specs=placed, out_specs=P(None, "seq", "tile", "grp"), check_vma=False
    )
```

```python
import functools
import math

import jax
import jax.numpy as jnp
from jax import lax
from jax.experimental import pallas as pl
from jax.experimental.pallas import tpu as pltpu
from jax.sharding import PartitionSpec as P

HEAD = 128
HEADS_TILE = 6
PLACE = (0, 1, 2, 3, 4, 5)
EPS = 1e-06
LOW = -1e30
EXP2_SCALE = HEAD ** (-0.5) * math.log2(math.e)
MESH = pl.DeviceIdType.MESH
BF16 = jnp.bfloat16
F32 = jnp.float32
NT = (((1,), (1,)), ((), ()))


def iota(shape, dim):
    return lax.broadcasted_iota(jnp.int32, shape, dim)


def one_hot(mask):
    return jnp.where(mask, 1.0, 0.0).astype(BF16)


def dot(a, b):
    return jnp.dot(a, b, preferred_element_type=F32)


def kernel(
    q_hbm, k_hbm, v_hbm, stretch_hbm, wb_hbm, lat_hbm, wq_hbm, wk_hbm, wv_hbm, out_hbm,
    stretch, q_buf, k_buf, v_buf, s_buf, w_buf, m_ref, l_ref, acc_ref, o_buf, a_buf, wb, wq, wk, wv,
    lat, lat_sq, lat_q, lat_k, lat_v, edge_out, p_own, p_send, p_recv, cond, tok, out_buf,
    first_send, first_recv, own_send, fwd_send, relay_send, second_recv, ret_send, ret_recv,
    tile_send, tile_recv, cond_send, cond_recv, row_send, row_recv, col_send, col_recv,
    load_sem, out_sem, near_sem,
):
    g, s, t = (lax.axis_index(name) for name in ("grp", "seq", "tile"))
    zl, c = g // 2, g % 2
    y, zh = s // 4, s % 4
    z = zh * 2 + zl
    sib = zl * 2 + (1 - c)
    head, working = (z + 8 - PLACE[0]) % 8, (z + 8 - PLACE[0]) % 8 < HEADS_TILE
    s_up, s_down = (s + 1) % 16, (s + 15) % 16

    def dev(grp, seq, tile=t):
        return {"grp": grp, "seq": seq, "tile": tile}

    def remote(src, dst, send, recv, to):
        return pltpu.make_async_remote_copy(
            src_ref=src, dst_ref=dst, send_sem=send, recv_sem=recv, device_id=to, device_id_type=MESH
        )

    def landed(ref, sem):
        pltpu.make_async_copy(ref, ref, sem).wait()

    partners = [dev(((z + i) % 8) % 2 * 2 + c, y * 4 + ((z + i) % 8) // 2) for i in range(1, 8)]
    partners += [dev(g, (y + i) % 4 * 4 + zh) for i in (1, 3)] + [dev(sib, s)]
    partners += [dev(g, s, (t + i) % 4) for i in range(1, 4)]
    barrier = pltpu.get_barrier_semaphore()
    for partner in partners:
        pl.semaphore_signal(barrier, inc=1, device_id=partner, device_id_type=MESH)
    pl.semaphore_wait(barrier, len(partners))

    first = ((k_hbm, k_buf.at[g, s]), (v_hbm, v_buf.at[g, s]), (q_hbm, q_buf.at[zl, zh]))

    def first_copy(i, h):
        src = first[i][0].at[:, h * HEAD:(h + 1) * HEAD]
        return remote(
            src, first[i][1], first_send.at[i, h], first_recv.at[i, zl, zh],
            dev(PLACE[h] % 2 * 2 + c, y * 4 + PLACE[h] // 2),
        )

    for i in range(3):
        for h in range(HEADS_TILE):
            @pl.when(z != PLACE[h])
            def _():
                first_copy(i, h).start()

            @pl.when(z == PLACE[h])
            def _():
                pltpu.make_async_copy(
                    first[i][0].at[:, h * HEAD:(h + 1) * HEAD], first[i][1], first_recv.at[i, zl, zh]
                ).start()

    loads = [
        pltpu.make_async_copy(src, dst, load_sem.at[i])
        for i, (src, dst) in enumerate((
            (stretch_hbm, stretch), (lat_hbm, lat.at[:, 32:96]), (wk_hbm, wk), (wv_hbm, wv), (wq_hbm, wq), (wb_hbm, wb),
        ))
    ]
    for load in loads:
        load.start()

    y_up, y_down, y_far = (y + 1) % 4, (y + 3) % 4, (y + 2) % 4
    for other in (y_up, y_down):
        pl.semaphore_signal(near_sem, inc=1, device_id=dev(g, other * 4 + zh), device_id_type=MESH)
    pl.semaphore_wait(near_sem, 2)

    mine, theirs = pl.ds(2 * c, 2), pl.ds(2 * (1 - c), 2)
    row_copies = [
        remote(lat_hbm.at[mine, 32:64], lat.at[mine, 0:32], row_send.at[0], row_recv.at[0], dev(g, s_up)),
        remote(lat_hbm.at[mine, 0:32], lat.at[mine, 96:128], row_send.at[1], row_recv.at[1], dev(g, s_down)),
    ]
    for copy in row_copies:
        copy.start()

    def project(refs, *pieces):
        cells = jnp.concatenate([lat[:, rows].reshape(-1, 1536) for rows in pieces], axis=0)
        wide = cells.astype(F32)
        squares = wide[:, :HEAD] * wide[:, :HEAD]
        for i in range(1, 12):
            lanes = slice(HEAD * i, HEAD * (i + 1))
            squares += wide[:, lanes] * wide[:, lanes]
        results = [(lat_sq, squares)] + [(ref, dot(cells, weight[...])) for weight, ref in refs]
        count = cells.shape[0] // len(pieces)
        for ref, result in results:
            for i, rows in enumerate(pieces):
                ref[:, rows] = result[count * i:count * (i + 1)].reshape(4, count // 4, -1)

    for load in loads[:5]:
        load.wait()
    project(((wk, lat_k), (wv, lat_v)), slice(32, 96))
    lat_q[...] = dot(lat[:, 32:96].reshape(256, 1536), wq[...]).reshape(4, 64, 384)

    bufs = (k_buf, v_buf)

    def region(kind, frame, row):
        return bufs[kind].at[frame, pl.ds(4 * row, 4)]

    def second(kind, frame, row, send, to):
        ref = region(kind, frame, row)
        return remote(ref, ref, send, second_recv.at[kind, frame, row], to)

    def low_of(i, frame):
        return jnp.where(stretch[frame] <= stretch[2 * i + c], 0.0, LOW)

    def score(row, core):
        for i in range(2):
            queries = q_buf[i].reshape(256, HEAD)
            top = m_ref[i]
            for part in range(2):
                frame = 2 * part + core
                keys = k_buf[frame, pl.ds(4 * row, 4)].reshape(256, HEAD)
                scores = lax.dot_general(queries, keys, NT, preferred_element_type=F32)
                s_buf[i, core * 4 + row, :, 256 * part:256 * (part + 1)] = scores
                top = jnp.maximum(top, jnp.maximum(scores[:, :HEAD], scores[:, HEAD:]) + low_of(i, frame))
            m_ref[i] = top

    def weigh(i):
        top = jnp.max(m_ref[i], axis=1, keepdims=True) * EXP2_SCALE
        m_ref[i] = jnp.broadcast_to(top, (256, HEAD))
        l_ref[i] = jnp.zeros((256, HEAD), F32)

        def block(j, carry):
            shift, total = m_ref[i], l_ref[i]
            for part in range(2):
                moved = shift - low_of(i, 2 * part + j // 4)
                for lane in range(2):
                    lanes = slice(256 * part + HEAD * lane, 256 * part + HEAD * (lane + 1))
                    weights = jnp.exp2(s_buf[i, j, :, lanes] * EXP2_SCALE - moved)
                    total += weights
                    w_buf[i, j, :, lanes] = weights.astype(BF16)
            l_ref[i] = total
            return carry

        lax.fori_loop(0, 8, block, 0)

    def blend(row, core):
        values = [v_buf[2 * part + core, pl.ds(4 * row, 4)].reshape(256, HEAD) for part in range(2)]
        values = jnp.concatenate(values, axis=0)
        for i in range(2):
            acc_ref[i] += dot(w_buf[i, core * 4 + row], values)

    def returned(i, j):
        return remote(o_buf.at[i, j], a_buf.at[head], ret_send.at[i, j], ret_recv.at[head], dev(2 * i + c, y * 4 + j))

    own_targets = [dev(g, y_up * 4 + zh), dev(g, y_down * 4 + zh), dev(sib, s)]
    far_rows = (y_down, y_up, y_far)

    def own_copy(kind, i, j):
        return second(kind, 2 * i + c, y, own_send.at[kind, i, j], own_targets[j])

    def forward_copy(kind, i):
        return second(kind, 2 * i + c, far_rows[i], fwd_send.at[kind, i], own_targets[i])

    def relay_copy(kind, i, j):
        return second(kind, 2 * i + c, far_rows[j], relay_send.at[j, kind, i], dev(sib, s))

    @pl.when(working)
    def _():
        m_ref[...] = jnp.full_like(m_ref, LOW)
        acc_ref[...] = jnp.zeros_like(acc_ref)

        for kind in range(2):
            for i in range(2):
                for j in range(4):
                    landed(bufs[kind].at[2 * i + c, 4 * y + j], first_recv.at[kind, i, j])
                for j in range(3):
                    own_copy(kind, i, j).start()
        for i in range(2):
            for j in range(4):
                landed(q_buf.at[i, j], first_recv.at[2, i, j])

        def relay(kind, j):
            for i in range(2):
                landed(region(kind, 2 * i + c, far_rows[j]), second_recv.at[kind, 2 * i + c, far_rows[j]])
                if i == j:
                    forward_copy(kind, i).start()
                relay_copy(kind, i, j).start()

        def from_sibling(kind, row):
            for i in range(2):
                frame = 2 * i + 1 - c
                landed(region(kind, frame, row), second_recv.at[kind, frame, row])

        score(y, c)
        for j in range(2):
            relay(0, j)
        from_sibling(0, y)
        score(y, 1 - c)
        score(y_down, c)
        score(y_up, c)
        for j in range(2):
            relay(1, j)
        relay(0, 2)
        for row in (y_down, y_up):
            from_sibling(0, row)
            score(row, 1 - c)
        score(y_far, c)
        from_sibling(0, y_far)
        score(y_far, 1 - c)
        weigh(0)
        relay(1, 2)
        weigh(1)
        blend(y, c)
        from_sibling(1, y)
        blend(y, 1 - c)
        for row in far_rows:
            blend(row, c)
        for row in far_rows:
            from_sibling(1, row)
            blend(row, 1 - c)

        for i in range(2):
            total = jnp.sum(l_ref[i], axis=1, keepdims=True)
            o_buf[i] = (acc_ref[i] / total).astype(BF16).reshape(4, 64, HEAD)
            for j in range(4):
                @pl.when(z != 2 * j + i)
                def _():
                    returned(i, j).start()

                @pl.when(z == 2 * j + i)
                def _():
                    pltpu.make_async_copy(o_buf.at[i, j], a_buf.at[head], ret_recv.at[head]).start()

    row_relays = []
    for i, rows in enumerate((slice(0, 32), slice(96, 128))):
        landed(lat.at[mine, rows], row_recv.at[i])
        ref = lat.at[mine, rows]
        row_relays.append(remote(ref, ref, row_send.at[2 + i], row_recv.at[2 + i], dev(sib, s)))
        row_relays[-1].start()
    for i, rows in enumerate((slice(0, 32), slice(96, 128))):
        landed(lat.at[theirs, rows], row_recv.at[2 + i])
    edge_id, cell = iota((32, 128), 0), iota((32, 128), 1)
    edge_cell = ((edge_id >> 1) & 7) * 16 + (edge_id & 1) + jnp.where(edge_id < 16, 14, 0)
    chosen = one_hot(edge_cell == cell)
    for frame in range(4):
        edges = dot(chosen, lat[frame, 0:128]).astype(BF16)
        edge_out[0, frame], edge_out[1, frame] = edges[:16], edges[16:]
    sides = (slice(128, 144), slice(144, 160))
    col_copies = [
        remote(edge_out.at[i], lat.at[:, sides[i]], col_send.at[i], col_recv.at[i], dev(g, s, neighbour))
        for i, neighbour in enumerate(((t + 1) % 4, (t + 3) % 4))
    ]
    for copy in col_copies:
        copy.start()
    project(((wk, lat_k), (wv, lat_v)), slice(0, 32), slice(96, 128))

    loads[5].wait()
    for h in range(HEADS_TILE):
        landed(a_buf.at[h], ret_recv.at[h])
    attended = jnp.concatenate([a_buf[h] for h in range(HEADS_TILE)], axis=1)
    row_id, token = iota((256, 64), 0), iota((256, 64), 1)
    partial = jnp.zeros((256, 512), F32)
    for part in range(3):
        place = (row_id & 31) - 10 * part
        column = (row_id >> 6) * 8 - 1 + place
        fits = (place >= 0) & (place < 10) & (column >= 0) & (column < 32)
        chosen = one_hot(fits & (((row_id >> 5) & 1) * 32 + column == token))
        rows = dot(chosen, attended).astype(BF16)
        partial += dot(rows, wb[:, 512 * part:512 * (part + 1)])
    p_own[...] = partial.reshape(4, 64, 512)
    p_send[...] = partial.astype(BF16).reshape(4, 64, 512)
    tile_copies = [
        remote(
            p_send.at[(t + i) % 4], p_recv.at[i - 1], tile_send.at[i - 1], tile_recv.at[i - 1],
            dev(g, s, (t + i) % 4),
        )
        for i in range(1, 4)
    ]
    for copy in tile_copies:
        copy.start()

    for i in range(3):
        landed(p_recv.at[i], tile_recv.at[i])
    summed = p_own[t]
    for i in range(3):
        summed += p_recv[i].astype(F32)
    squares = summed * summed
    squares = squares[:, :128] + squares[:, 128:256] + squares[:, 256:384] + squares[:, 384:]
    left, right = iota((64, 64), 0), iota((64, 64), 1)

    def token_of(row):
        place = row & 31
        return place - jnp.where(place >= 10, 10, 0) - jnp.where(place >= 20, 10, 0)

    same = ((left >> 5) == (right >> 5)) & (token_of(left) == token_of(right))
    together = jnp.dot(
        jnp.where(same, 1.0, 0.0), squares, preferred_element_type=F32, precision=lax.Precision.HIGHEST
    )
    mean = jnp.sum(together, axis=1, keepdims=True) * (1.0 / 1536)
    cond[g, 1:3] = (summed * lax.rsqrt(mean + EPS)).astype(BF16).reshape(2, 32, 512)

    slots = (slice(1, 3), slice(0, 1), slice(3, 4))

    def cond_copy(frame, src, slot, sem, to):
        return remote(cond.at[frame, src], cond.at[frame, slots[slot]], cond_send.at[sem], cond_recv.at[frame, slot], to)

    across = (1 - zl) * 2 + c
    cond_copies = [
        cond_copy(g, slots[0], 0, 0, dev(across, s)),
        cond_copy(g, slice(2, 3), 1, 1, dev(c, s_up)),
        cond_copy(g, slice(2, 3), 1, 2, dev(2 + c, s_up)),
        cond_copy(g, slice(1, 2), 2, 3, dev(c, s_down)),
        cond_copy(g, slice(1, 2), 2, 4, dev(2 + c, s_down)),
        cond_copy(g, slots[0], 0, 5, dev(sib, s)),
    ]
    for copy in cond_copies:
        copy.start()
    for i in range(2):
        landed(lat.at[:, sides[i]], col_recv.at[i])
    project(((wk, lat_k), (wv, lat_v)), slice(128, 160))
    arrivals = [((1 - zl) * 2 + c, 0), (c, 1), (2 + c, 1), (c, 2), (2 + c, 2)]
    for i, (frame, slot) in enumerate(arrivals):
        landed(cond.at[frame, slots[slot]], cond_recv.at[frame, slot])
        cond_copies.append(cond_copy(frame, slots[slot], slot, 6 + i, dev(sib, s)))
        cond_copies[-1].start()

    place, source = iota((64, 128), 0), iota((64, 128), 1)
    unpack = [
        one_hot(((place & 15) < 10) & ((place >> 4) * 32 + 10 * part + (place & 15) == source)) for part in range(3)
    ]
    cell, source = iota((160, 64), 0), iota((160, 64), 1)
    side = cell - 128
    cell_row = jnp.where(cell < 128, cell >> 4, (side >> 1) & 7)
    cell_token = jnp.where(cell < 128, 1 + ((cell & 15) >> 1), jnp.where(side < 16, 0, 9))
    above = (cell_row >> 1) * 16 + cell_token == source
    spread = one_hot(above)
    diagonal = iota((64, 64), 0) == iota((64, 64), 1)

    query, key = iota((64, 160), 0), iota((64, 160), 1)
    side = key - 128
    key_row = jnp.where(key < 128, key >> 4, (side >> 1) & 7)
    key_col = jnp.where(key < 128, 2 + (key & 15), (side & 1) + jnp.where(side < 16, 0, 18))
    row_off, col_off = key_row - (query >> 4) - 2, key_col - (query & 15) - 2
    row_at, col_at = 4 * s - 2 + key_row, 16 * t - 2 + key_col
    near = (jnp.abs(row_off) <= 2) & (jnp.abs(col_off) <= 2)
    near = near & (row_at >= 0) & (row_at < 64) & (col_at >= 0) & (col_at < 64)
    low = jnp.where(near, 0.0, LOW)

    def layer(core):
        for i in range(2):
            rows = cond[2 * i + core].reshape(128, 512)
            for part in range(3):
                tok[i, :, 512 * part:512 * (part + 1)] = dot(unpack[part], rows).astype(BF16)
        tokens = tok[...].reshape(128, 1536)
        parts = [dot(tokens, weight[...]).astype(BF16) for weight in (wk, wv, wq)]
        scores, blocks = [], []
        for i in range(2):
            frame = 2 * i + core
            pair = lax.dot_general(tok[i], tok[i], NT, preferred_element_type=F32)
            token_sq = jnp.sum(jnp.where(diagonal, pair, 0.0), axis=0, keepdims=True)
            cross = lax.dot_general(lat[frame], tok[i], NT, preferred_element_type=F32)
            square = jnp.sum(jnp.where(above, 2.0 * cross + token_sq, 0.0), axis=1, keepdims=True)
            square = jnp.maximum(square + jnp.sum(lat_sq[frame], axis=1, keepdims=True), 0.0)
            scale = lax.rsqrt(square * (1.0 / 1536) + EPS)
            keys, values = (
                (scale * (ref[frame] + dot(spread, part[64 * i:64 * (i + 1)]))).astype(BF16)
                for ref, part in ((lat_k, parts[0]), (lat_v, parts[1]))
            )
            queries = dot(spread[32:96], parts[2][64 * i:64 * (i + 1)])
            queries = (scale[32:96] * (lat_q[frame] + queries)).astype(BF16)
            for h in range(3):
                lanes = slice(h * HEAD, (h + 1) * HEAD)
                score = lax.dot_general(queries[:, lanes], keys[:, lanes], NT, preferred_element_type=F32)
                scores.append(score * HEAD ** (-0.5) + low)
                blocks.append((frame, lanes, values[:, lanes]))
        scores = jnp.concatenate(scores, axis=0)
        unscaled = jnp.exp(scores - jnp.max(scores, axis=1, keepdims=True))
        weights = (unscaled * (1.0 / jnp.sum(unscaled, axis=1, keepdims=True))).astype(BF16)
        for i, (frame, lanes, values) in enumerate(blocks):
            blended = dot(weights[64 * i:64 * (i + 1)], values).astype(BF16)
            out_buf[frame, :, :, lanes] = blended.reshape(4, 16, HEAD)

    layer(c)
    for frame, slot in [(sib, 0)] + [(2 * i + 1 - c, slot) for i, slot in ((0, 1), (1, 1), (0, 2), (1, 2))] + [((1 - zl) * 2 + 1 - c, 0)]:
        landed(cond.at[frame, slots[slot]], cond_recv.at[frame, slot])
    layer(1 - c)
    result = pltpu.make_async_copy(out_buf, out_hbm, out_sem)
    result.start()

    for i in range(3):
        for h in range(HEADS_TILE):
            @pl.when(z != PLACE[h])
            def _():
                first_copy(i, h).wait_send()
    @pl.when(working)
    def _():
        for kind in range(2):
            for i in range(2):
                for j in range(3):
                    own_copy(kind, i, j).wait_send()
                    relay_copy(kind, i, j).wait_send()
                forward_copy(kind, i).wait_send()
        for i in range(2):
            for j in range(4):
                @pl.when(z != 2 * j + i)
                def _():
                    returned(i, j).wait_send()

    for copy in row_copies + row_relays + tile_copies + col_copies + cond_copies:
        copy.wait_send()
    result.wait()


def local(base_q, base_k, base_v, frame_stretch, bridge_w, sr_latent, sr_wq, sr_wk, sr_wv):
    hbm = pl.BlockSpec(memory_space=pltpu.HBM)
    dma = pltpu.SemaphoreType.DMA
    vmem = pltpu.VMEM
    call = pl.pallas_call(
        kernel,
        out_shape=jax.ShapeDtypeStruct((4, 4, 16, 384), BF16),
        in_specs=[hbm] * 9,
        out_specs=hbm,
        scratch_shapes=[
            pltpu.SMEM((4,), jnp.int32),
            vmem((2, 4, 64, HEAD), BF16),
            vmem((4, 16, 64, HEAD), BF16),
            vmem((4, 16, 64, HEAD), BF16),
            vmem((2, 8, 256, 512), F32),
            vmem((2, 8, 256, 512), BF16),
            vmem((2, 256, HEAD), F32),
            vmem((2, 256, HEAD), F32),
            vmem((2, 256, HEAD), F32),
            vmem((2, 4, 64, HEAD), BF16),
            vmem((HEADS_TILE, 64, HEAD), BF16),
            vmem((768, 1536), BF16),
            vmem((1536, 384), BF16),
            vmem((1536, 384), BF16),
            vmem((1536, 384), BF16),
            vmem((4, 160, 1536), BF16),
            vmem((4, 160, HEAD), F32),
            vmem((4, 64, 384), F32),
            vmem((4, 160, 384), F32),
            vmem((4, 160, 384), F32),
            vmem((2, 4, 16, 1536), BF16),
            vmem((4, 64, 512), F32),
            vmem((4, 64, 512), BF16),
            vmem((3, 64, 512), BF16),
            vmem((4, 4, 32, 512), BF16),
            vmem((2, 64, 1536), BF16),
            vmem((4, 4, 16, 384), BF16),
            dma((3, HEADS_TILE)),
            dma((3, 2, 4)),
            dma((2, 2, 3)),
            dma((2, 2)),
            dma((3, 2, 2)),
            dma((2, 4, 4)),
            dma((2, 4)),
            dma((HEADS_TILE,)),
            dma((3,)),
            dma((3,)),
            dma((11,)),
            dma((4, 3)),
            dma((4,)),
            dma((4,)),
            dma((2,)),
            dma((2,)),
            dma((6,)),
            dma,
            pltpu.SemaphoreType.REGULAR,
        ],
        compiler_params=pltpu.CompilerParams(
            collective_id=0, has_side_effects=True, vmem_limit_bytes=62 * 1024 * 1024
        ),
        cost_estimate=pl.CostEstimate(flops=4 * 10**9, bytes_accessed=16 * 2**20, transcendentals=2 * 10**6),
    )
    return call(
        base_q.reshape(64, 768), base_k.reshape(64, 768), base_v.reshape(64, 768), frame_stretch,
        bridge_w, sr_latent.reshape(4, 64, 1536), sr_wq, sr_wk, sr_wv,
    )


def solution(mesh):
    placed = (
        P("grp", "seq", None, "tile"),
        P("grp", "seq", None, "tile"),
        P("grp", "seq", None, "tile"),
        P(),
        P("tile", None),
        P(None, "seq", "tile", None),
        P(None, "grp"),
        P(None, "grp"),
        P(None, "grp"),
    )
    return jax.shard_map(
        local, mesh=mesh, in_specs=placed, out_specs=P(None, "seq", "tile", "grp"), check_vma=False
    )
```

```python
import functools
import math

import jax
import jax.numpy as jnp
from jax import lax
from jax.experimental import pallas as pl
from jax.experimental.pallas import tpu as pltpu
from jax.sharding import PartitionSpec as P

HEAD = 128
HEADS_TILE = 6
PLACE = (0, 1, 2, 3, 4, 5)
EPS = 1e-06
LOW = -1e30
EXP2_SCALE = HEAD ** (-0.5) * math.log2(math.e)
MESH = pl.DeviceIdType.MESH
BF16 = jnp.bfloat16
F32 = jnp.float32
NT = (((1,), (1,)), ((), ()))


def iota(shape, dim):
    return lax.broadcasted_iota(jnp.int32, shape, dim)


def one_hot(mask):
    return jnp.where(mask, 1.0, 0.0).astype(BF16)


def dot(a, b):
    return jnp.dot(a, b, preferred_element_type=F32)


def kernel(
    q_hbm, k_hbm, v_hbm, stretch_hbm, wb_hbm, lat_hbm, wq_hbm, wk_hbm, wv_hbm, out_hbm,
    stretch, q_buf, k_buf, v_buf, s_buf, w_buf, m_ref, l_ref, acc_ref, o_buf, a_buf, wb, wq, wk, wv,
    lat, lat_sq, lat_q, lat_k, lat_v, edge_out, p_own, p_send, p_recv, cond, tok, out_buf,
    first_send, first_recv, own_send, fwd_send, relay_send, second_recv, ret_send, ret_recv,
    tile_send, tile_recv, cond_send, cond_recv, row_send, row_recv, col_send, col_recv,
    load_sem, out_sem, near_sem,
):
    g, s, t = (lax.axis_index(name) for name in ("grp", "seq", "tile"))
    zl, c = g // 2, g % 2
    y, zh = s // 4, s % 4
    z = zh * 2 + zl
    sib = zl * 2 + (1 - c)
    head, working = (z + 8 - PLACE[0]) % 8, (z + 8 - PLACE[0]) % 8 < HEADS_TILE
    s_up, s_down = (s + 1) % 16, (s + 15) % 16

    def dev(grp, seq, tile=t):
        return {"grp": grp, "seq": seq, "tile": tile}

    def remote(src, dst, send, recv, to):
        return pltpu.make_async_remote_copy(
            src_ref=src, dst_ref=dst, send_sem=send, recv_sem=recv, device_id=to, device_id_type=MESH
        )

    def landed(ref, sem):
        pltpu.make_async_copy(ref, ref, sem).wait()

    partners = [dev(((z + i) % 8) % 2 * 2 + c, y * 4 + ((z + i) % 8) // 2) for i in range(1, 8)]
    partners += [dev(g, (y + i) % 4 * 4 + zh) for i in (1, 3)] + [dev(sib, s)]
    partners += [dev(g, s, (t + i) % 4) for i in range(1, 4)]
    barrier = pltpu.get_barrier_semaphore()
    for partner in partners:
        pl.semaphore_signal(barrier, inc=1, device_id=partner, device_id_type=MESH)
    pl.semaphore_wait(barrier, len(partners))

    first = ((k_hbm, k_buf.at[g, s]), (v_hbm, v_buf.at[g, s]), (q_hbm, q_buf.at[zl, zh]))

    def first_copy(i, h):
        src = first[i][0].at[:, h * HEAD:(h + 1) * HEAD]
        return remote(
            src, first[i][1], first_send.at[i, h], first_recv.at[i, zl, zh],
            dev(PLACE[h] % 2 * 2 + c, y * 4 + PLACE[h] // 2),
        )

    for i in range(3):
        for h in range(HEADS_TILE):
            @pl.when(z != PLACE[h])
            def _():
                first_copy(i, h).start()

            @pl.when(z == PLACE[h])
            def _():
                pltpu.make_async_copy(
                    first[i][0].at[:, h * HEAD:(h + 1) * HEAD], first[i][1], first_recv.at[i, zl, zh]
                ).start()

    loads = [
        pltpu.make_async_copy(src, dst, load_sem.at[i])
        for i, (src, dst) in enumerate((
            (stretch_hbm, stretch), (lat_hbm, lat.at[:, 32:96]), (wk_hbm, wk), (wv_hbm, wv), (wq_hbm, wq), (wb_hbm, wb),
        ))
    ]
    for load in loads:
        load.start()

    y_up, y_down, y_far = (y + 1) % 4, (y + 3) % 4, (y + 2) % 4
    for other in (y_up, y_down):
        pl.semaphore_signal(near_sem, inc=1, device_id=dev(g, other * 4 + zh), device_id_type=MESH)
    pl.semaphore_wait(near_sem, 2)

    mine, theirs = pl.ds(2 * c, 2), pl.ds(2 * (1 - c), 2)
    row_copies = [
        remote(lat_hbm.at[mine, 32:64], lat.at[mine, 0:32], row_send.at[0], row_recv.at[0], dev(g, s_up)),
        remote(lat_hbm.at[mine, 0:32], lat.at[mine, 96:128], row_send.at[1], row_recv.at[1], dev(g, s_down)),
    ]
    for copy in row_copies:
        copy.start()

    def project(refs, *pieces):
        cells = jnp.concatenate([lat[:, rows].reshape(-1, 1536) for rows in pieces], axis=0)
        wide = cells.astype(F32)
        squares = wide[:, :HEAD] * wide[:, :HEAD]
        for i in range(1, 12):
            lanes = slice(HEAD * i, HEAD * (i + 1))
            squares += wide[:, lanes] * wide[:, lanes]
        results = [(lat_sq, squares)] + [(ref, dot(cells, weight[...])) for weight, ref in refs]
        count = cells.shape[0] // len(pieces)
        for ref, result in results:
            for i, rows in enumerate(pieces):
                ref[:, rows] = result[count * i:count * (i + 1)].reshape(4, count // 4, -1)

    for load in loads[:5]:
        load.wait()
    project(((wk, lat_k), (wv, lat_v)), slice(32, 96))
    lat_q[...] = dot(lat[:, 32:96].reshape(256, 1536), wq[...]).reshape(4, 64, 384)

    bufs = (k_buf, v_buf)

    def region(kind, frame, row):
        return bufs[kind].at[frame, pl.ds(4 * row, 4)]

    def second(kind, frame, row, send, to):
        ref = region(kind, frame, row)
        return remote(ref, ref, send, second_recv.at[kind, frame, row], to)

    def low_of(i, frame):
        return jnp.where(stretch[frame] <= stretch[2 * i + c], 0.0, LOW)

    def score(row, core):
        for i in range(2):
            queries = q_buf[i].reshape(256, HEAD)
            top = m_ref[i]
            for part in range(2):
                frame = 2 * part + core
                keys = k_buf[frame, pl.ds(4 * row, 4)].reshape(256, HEAD)
                scores = lax.dot_general(queries, keys, NT, preferred_element_type=F32)
                s_buf[i, core * 4 + row, :, 256 * part:256 * (part + 1)] = scores
                top = jnp.maximum(top, jnp.maximum(scores[:, :HEAD], scores[:, HEAD:]) + low_of(i, frame))
            m_ref[i] = top

    def weigh(i):
        top = jnp.max(m_ref[i], axis=1, keepdims=True) * EXP2_SCALE
        m_ref[i] = jnp.broadcast_to(top, (256, HEAD))
        l_ref[i] = jnp.zeros((256, HEAD), F32)

        def block(j, carry):
            shift, total = m_ref[i], l_ref[i]
            for part in range(2):
                moved = shift - low_of(i, 2 * part + j // 4)
                for lane in range(2):
                    lanes = slice(256 * part + HEAD * lane, 256 * part + HEAD * (lane + 1))
                    weights = jnp.exp2(s_buf[i, j, :, lanes] * EXP2_SCALE - moved)
                    total += weights
                    w_buf[i, j, :, lanes] = weights.astype(BF16)
            l_ref[i] = total
            return carry

        lax.fori_loop(0, 8, block, 0)

    def blend(row, core):
        values = [v_buf[2 * part + core, pl.ds(4 * row, 4)].reshape(256, HEAD) for part in range(2)]
        values = jnp.concatenate(values, axis=0)
        for i in range(2):
            acc_ref[i] += dot(w_buf[i, core * 4 + row], values)

    def returned(i, j):
        return remote(o_buf.at[i, j], a_buf.at[head], ret_send.at[i, j], ret_recv.at[head], dev(2 * i + c, y * 4 + j))

    own_targets = [dev(g, y_up * 4 + zh), dev(g, y_down * 4 + zh), dev(sib, s)]
    far_rows = (y_down, y_up, y_far)

    def own_copy(kind, i, j):
        return second(kind, 2 * i + c, y, own_send.at[kind, i, j], own_targets[j])

    def forward_copy(kind, i):
        return second(kind, 2 * i + c, far_rows[i], fwd_send.at[kind, i], own_targets[i])

    def relay_copy(kind, i, j):
        return second(kind, 2 * i + c, far_rows[j], relay_send.at[j, kind, i], dev(sib, s))

    @pl.when(working)
    def _():
        m_ref[...] = jnp.full_like(m_ref, LOW)
        acc_ref[...] = jnp.zeros_like(acc_ref)

        for kind in range(2):
            for i in range(2):
                for j in range(4):
                    landed(bufs[kind].at[2 * i + c, 4 * y + j], first_recv.at[kind, i, j])
                own_copy(kind, i, i).start()
            for i, j in ((1, 0), (0, 1), (0, 2), (1, 2)):
                own_copy(kind, i, j).start()
        for i in range(2):
            for j in range(4):
                landed(q_buf.at[i, j], first_recv.at[2, i, j])

        def relay(kind, j):
            for i in range(2):
                landed(region(kind, 2 * i + c, far_rows[j]), second_recv.at[kind, 2 * i + c, far_rows[j]])
                if i == j:
                    forward_copy(kind, i).start()
                relay_copy(kind, i, j).start()

        def from_sibling(kind, row):
            for i in range(2):
                frame = 2 * i + 1 - c
                landed(region(kind, frame, row), second_recv.at[kind, frame, row])

        score(y, c)
        for j in range(2):
            relay(0, j)
        from_sibling(0, y)
        score(y, 1 - c)
        score(y_down, c)
        score(y_up, c)
        for j in range(2):
            relay(1, j)
        relay(0, 2)
        for row in (y_down, y_up):
            from_sibling(0, row)
            score(row, 1 - c)
        score(y_far, c)
        from_sibling(0, y_far)
        score(y_far, 1 - c)
        weigh(0)
        weigh(1)
        blend(y, c)
        from_sibling(1, y)
        blend(y, 1 - c)
        blend(y_down, c)
        blend(y_up, c)
        relay(1, 2)
        for row in (y_down, y_up):
            from_sibling(1, row)
            blend(row, 1 - c)
        blend(y_far, c)
        from_sibling(1, y_far)
        blend(y_far, 1 - c)

        for i in range(2):
            total = jnp.sum(l_ref[i], axis=1, keepdims=True)
            o_buf[i] = (acc_ref[i] / total).astype(BF16).reshape(4, 64, HEAD)
            for j in range(4):
                @pl.when(z != 2 * j + i)
                def _():
                    returned(i, j).start()

                @pl.when(z == 2 * j + i)
                def _():
                    pltpu.make_async_copy(o_buf.at[i, j], a_buf.at[head], ret_recv.at[head]).start()

    row_relays = []
    for i, rows in enumerate((slice(0, 32), slice(96, 128))):
        landed(lat.at[mine, rows], row_recv.at[i])
        ref = lat.at[mine, rows]
        row_relays.append(remote(ref, ref, row_send.at[2 + i], row_recv.at[2 + i], dev(sib, s)))
        row_relays[-1].start()
    for i, rows in enumerate((slice(0, 32), slice(96, 128))):
        landed(lat.at[theirs, rows], row_recv.at[2 + i])
    edge_id, cell = iota((32, 128), 0), iota((32, 128), 1)
    edge_cell = ((edge_id >> 1) & 7) * 16 + (edge_id & 1) + jnp.where(edge_id < 16, 14, 0)
    chosen = one_hot(edge_cell == cell)
    for frame in range(4):
        edges = dot(chosen, lat[frame, 0:128]).astype(BF16)
        edge_out[0, frame], edge_out[1, frame] = edges[:16], edges[16:]
    sides = (slice(128, 144), slice(144, 160))
    col_copies = [
        remote(edge_out.at[i], lat.at[:, sides[i]], col_send.at[i], col_recv.at[i], dev(g, s, neighbour))
        for i, neighbour in enumerate(((t + 1) % 4, (t + 3) % 4))
    ]
    for copy in col_copies:
        copy.start()
    project(((wk, lat_k), (wv, lat_v)), slice(0, 32), slice(96, 128))

    loads[5].wait()
    for h in range(HEADS_TILE):
        landed(a_buf.at[h], ret_recv.at[h])
    attended = jnp.concatenate([a_buf[h] for h in range(HEADS_TILE)], axis=1)
    row_id, token = iota((256, 64), 0), iota((256, 64), 1)
    partial = jnp.zeros((256, 512), F32)
    for part in range(3):
        place = (row_id & 31) - 10 * part
        column = (row_id >> 6) * 8 - 1 + place
        fits = (place >= 0) & (place < 10) & (column >= 0) & (column < 32)
        chosen = one_hot(fits & (((row_id >> 5) & 1) * 32 + column == token))
        rows = dot(chosen, attended).astype(BF16)
        partial += dot(rows, wb[:, 512 * part:512 * (part + 1)])
    p_own[...] = partial.reshape(4, 64, 512)
    p_send[...] = partial.astype(BF16).reshape(4, 64, 512)
    tile_copies = [
        remote(
            p_send.at[(t + i) % 4], p_recv.at[i - 1], tile_send.at[i - 1], tile_recv.at[i - 1],
            dev(g, s, (t + i) % 4),
        )
        for i in (2, 1, 3)
    ]
    for copy in tile_copies:
        copy.start()

    for i in range(3):
        landed(p_recv.at[i], tile_recv.at[i])
    summed = p_own[t]
    for i in range(3):
        summed += p_recv[i].astype(F32)
    squares = summed * summed
    squares = squares[:, :128] + squares[:, 128:256] + squares[:, 256:384] + squares[:, 384:]
    left, right = iota((64, 64), 0), iota((64, 64), 1)

    def token_of(row):
        place = row & 31
        return place - jnp.where(place >= 10, 10, 0) - jnp.where(place >= 20, 10, 0)

    same = ((left >> 5) == (right >> 5)) & (token_of(left) == token_of(right))
    together = jnp.dot(
        jnp.where(same, 1.0, 0.0), squares, preferred_element_type=F32, precision=lax.Precision.HIGHEST
    )
    mean = jnp.sum(together, axis=1, keepdims=True) * (1.0 / 1536)
    cond[g, 1:3] = (summed * lax.rsqrt(mean + EPS)).astype(BF16).reshape(2, 32, 512)

    slots = (slice(1, 3), slice(0, 1), slice(3, 4))

    def cond_copy(frame, src, slot, sem, to):
        return remote(cond.at[frame, src], cond.at[frame, slots[slot]], cond_send.at[sem], cond_recv.at[frame, slot], to)

    across = (1 - zl) * 2 + c
    cond_copies = [
        cond_copy(g, slots[0], 0, 0, dev(across, s)),
        cond_copy(g, slice(2, 3), 1, 1, dev(c, s_up)),
        cond_copy(g, slice(2, 3), 1, 2, dev(2 + c, s_up)),
        cond_copy(g, slice(1, 2), 2, 3, dev(c, s_down)),
        cond_copy(g, slice(1, 2), 2, 4, dev(2 + c, s_down)),
        cond_copy(g, slots[0], 0, 5, dev(sib, s)),
    ]
    for copy in cond_copies:
        copy.start()
    for i in range(2):
        landed(lat.at[:, sides[i]], col_recv.at[i])
    project(((wk, lat_k), (wv, lat_v)), slice(128, 160))
    arrivals = [((1 - zl) * 2 + c, 0), (c, 1), (2 + c, 1), (c, 2), (2 + c, 2)]
    for i, (frame, slot) in enumerate(arrivals):
        landed(cond.at[frame, slots[slot]], cond_recv.at[frame, slot])
        cond_copies.append(cond_copy(frame, slots[slot], slot, 6 + i, dev(sib, s)))
        cond_copies[-1].start()

    place, source = iota((64, 128), 0), iota((64, 128), 1)
    unpack = [
        one_hot(((place & 15) < 10) & ((place >> 4) * 32 + 10 * part + (place & 15) == source)) for part in range(3)
    ]
    cell, source = iota((160, 64), 0), iota((160, 64), 1)
    side = cell - 128
    cell_row = jnp.where(cell < 128, cell >> 4, (side >> 1) & 7)
    cell_token = jnp.where(cell < 128, 1 + ((cell & 15) >> 1), jnp.where(side < 16, 0, 9))
    above = (cell_row >> 1) * 16 + cell_token == source
    spread = one_hot(above)
    diagonal = iota((64, 64), 0) == iota((64, 64), 1)

    query, key = iota((64, 160), 0), iota((64, 160), 1)
    side = key - 128
    key_row = jnp.where(key < 128, key >> 4, (side >> 1) & 7)
    key_col = jnp.where(key < 128, 2 + (key & 15), (side & 1) + jnp.where(side < 16, 0, 18))
    row_off, col_off = key_row - (query >> 4) - 2, key_col - (query & 15) - 2
    row_at, col_at = 4 * s - 2 + key_row, 16 * t - 2 + key_col
    near = (jnp.abs(row_off) <= 2) & (jnp.abs(col_off) <= 2)
    near = near & (row_at >= 0) & (row_at < 64) & (col_at >= 0) & (col_at < 64)
    low = jnp.where(near, 0.0, LOW)

    def layer(core):
        for i in range(2):
            rows = cond[2 * i + core].reshape(128, 512)
            for part in range(3):
                tok[i, :, 512 * part:512 * (part + 1)] = dot(unpack[part], rows).astype(BF16)
        tokens = tok[...].reshape(128, 1536)
        parts = [dot(tokens, weight[...]).astype(BF16) for weight in (wk, wv, wq)]
        scores, blocks = [], []
        for i in range(2):
            frame = 2 * i + core
            pair = lax.dot_general(tok[i], tok[i], NT, preferred_element_type=F32)
            token_sq = jnp.sum(jnp.where(diagonal, pair, 0.0), axis=0, keepdims=True)
            cross = lax.dot_general(lat[frame], tok[i], NT, preferred_element_type=F32)
            square = jnp.sum(jnp.where(above, 2.0 * cross + token_sq, 0.0), axis=1, keepdims=True)
            square = jnp.maximum(square + jnp.sum(lat_sq[frame], axis=1, keepdims=True), 0.0)
            scale = lax.rsqrt(square * (1.0 / 1536) + EPS)
            keys, values = (
                (scale * (ref[frame] + dot(spread, part[64 * i:64 * (i + 1)]))).astype(BF16)
                for ref, part in ((lat_k, parts[0]), (lat_v, parts[1]))
            )
            queries = dot(spread[32:96], parts[2][64 * i:64 * (i + 1)])
            queries = (scale[32:96] * (lat_q[frame] + queries)).astype(BF16)
            for h in range(3):
                lanes = slice(h * HEAD, (h + 1) * HEAD)
                score = lax.dot_general(queries[:, lanes], keys[:, lanes], NT, preferred_element_type=F32)
                scores.append(score * HEAD ** (-0.5) + low)
                blocks.append((frame, lanes, values[:, lanes]))
        scores = jnp.concatenate(scores, axis=0)
        unscaled = jnp.exp(scores - jnp.max(scores, axis=1, keepdims=True))
        weights = (unscaled * (1.0 / jnp.sum(unscaled, axis=1, keepdims=True))).astype(BF16)
        for i, (frame, lanes, values) in enumerate(blocks):
            blended = dot(weights[64 * i:64 * (i + 1)], values).astype(BF16)
            out_buf[frame, :, :, lanes] = blended.reshape(4, 16, HEAD)

    layer(c)
    for frame, slot in [(sib, 0)] + [(2 * i + 1 - c, slot) for i, slot in ((0, 1), (1, 1), (0, 2), (1, 2))] + [((1 - zl) * 2 + 1 - c, 0)]:
        landed(cond.at[frame, slots[slot]], cond_recv.at[frame, slot])
    layer(1 - c)
    result = pltpu.make_async_copy(out_buf, out_hbm, out_sem)
    result.start()

    for i in range(3):
        for h in range(HEADS_TILE):
            @pl.when(z != PLACE[h])
            def _():
                first_copy(i, h).wait_send()
    @pl.when(working)
    def _():
        for kind in range(2):
            for i in range(2):
                for j in range(3):
                    own_copy(kind, i, j).wait_send()
                    relay_copy(kind, i, j).wait_send()
                forward_copy(kind, i).wait_send()
        for i in range(2):
            for j in range(4):
                @pl.when(z != 2 * j + i)
                def _():
                    returned(i, j).wait_send()

    for copy in row_copies + row_relays + tile_copies + col_copies + cond_copies:
        copy.wait_send()
    result.wait()


def local(base_q, base_k, base_v, frame_stretch, bridge_w, sr_latent, sr_wq, sr_wk, sr_wv):
    hbm = pl.BlockSpec(memory_space=pltpu.HBM)
    dma = pltpu.SemaphoreType.DMA
    vmem = pltpu.VMEM
    call = pl.pallas_call(
        kernel,
        out_shape=jax.ShapeDtypeStruct((4, 4, 16, 384), BF16),
        in_specs=[hbm] * 9,
        out_specs=hbm,
        scratch_shapes=[
            pltpu.SMEM((4,), jnp.int32),
            vmem((2, 4, 64, HEAD), BF16),
            vmem((4, 16, 64, HEAD), BF16),
            vmem((4, 16, 64, HEAD), BF16),
            vmem((2, 8, 256, 512), F32),
            vmem((2, 8, 256, 512), BF16),
            vmem((2, 256, HEAD), F32),
            vmem((2, 256, HEAD), F32),
            vmem((2, 256, HEAD), F32),
            vmem((2, 4, 64, HEAD), BF16),
            vmem((HEADS_TILE, 64, HEAD), BF16),
            vmem((768, 1536), BF16),
            vmem((1536, 384), BF16),
            vmem((1536, 384), BF16),
            vmem((1536, 384), BF16),
            vmem((4, 160, 1536), BF16),
            vmem((4, 160, HEAD), F32),
            vmem((4, 64, 384), F32),
            vmem((4, 160, 384), F32),
            vmem((4, 160, 384), F32),
            vmem((2, 4, 16, 1536), BF16),
            vmem((4, 64, 512), F32),
            vmem((4, 64, 512), BF16),
            vmem((3, 64, 512), BF16),
            vmem((4, 4, 32, 512), BF16),
            vmem((2, 64, 1536), BF16),
            vmem((4, 4, 16, 384), BF16),
            dma((3, HEADS_TILE)),
            dma((3, 2, 4)),
            dma((2, 2, 3)),
            dma((2, 2)),
            dma((3, 2, 2)),
            dma((2, 4, 4)),
            dma((2, 4)),
            dma((HEADS_TILE,)),
            dma((3,)),
            dma((3,)),
            dma((11,)),
            dma((4, 3)),
            dma((4,)),
            dma((4,)),
            dma((2,)),
            dma((2,)),
            dma((6,)),
            dma,
            pltpu.SemaphoreType.REGULAR,
        ],
        compiler_params=pltpu.CompilerParams(
            collective_id=0, has_side_effects=True, vmem_limit_bytes=62 * 1024 * 1024
        ),
        cost_estimate=pl.CostEstimate(flops=4 * 10**9, bytes_accessed=16 * 2**20, transcendentals=2 * 10**6),
    )
    return call(
        base_q.reshape(64, 768), base_k.reshape(64, 768), base_v.reshape(64, 768), frame_stretch,
        bridge_w, sr_latent.reshape(4, 64, 1536), sr_wq, sr_wk, sr_wv,
    )


def solution(mesh):
    placed = (
        P("grp", "seq", None, "tile"),
        P("grp", "seq", None, "tile"),
        P("grp", "seq", None, "tile"),
        P(),
        P("tile", None),
        P(None, "seq", "tile", None),
        P(None, "grp"),
        P(None, "grp"),
        P(None, "grp"),
    )
    return jax.shard_map(
        local, mesh=mesh, in_specs=placed, out_specs=P(None, "seq", "tile", "grp"), check_vma=False
    )
```

```python
import functools
import math

import jax
import jax.numpy as jnp
from jax import lax
from jax.experimental import pallas as pl
from jax.experimental.pallas import tpu as pltpu
from jax.sharding import PartitionSpec as P

HEAD = 128
HEADS_TILE = 6
PLACE = (0, 1, 2, 3, 4, 5)
EPS = 1e-06
LOW = -1e30
EXP2_SCALE = HEAD ** (-0.5) * math.log2(math.e)
MESH = pl.DeviceIdType.MESH
BF16 = jnp.bfloat16
F32 = jnp.float32
NT = (((1,), (1,)), ((), ()))


def iota(shape, dim):
    return lax.broadcasted_iota(jnp.int32, shape, dim)


def one_hot(mask):
    return jnp.where(mask, 1.0, 0.0).astype(BF16)


def dot(a, b):
    return jnp.dot(a, b, preferred_element_type=F32)


def kernel(
    q_hbm, k_hbm, v_hbm, stretch_hbm, wb_hbm, lat_hbm, wq_hbm, wk_hbm, wv_hbm, out_hbm,
    stretch, q_buf, k_buf, v_buf, s_buf, w_buf, m_ref, l_ref, acc_ref, o_buf, a_buf, wb, wq, wk, wv,
    lat, lat_sq, lat_q, lat_k, lat_v, edge_out, p_own, p_send, p_recv, cond, tok, out_buf,
    first_send, first_recv, own_send, fwd_send, relay_send, second_recv, ret_send, ret_recv,
    tile_send, tile_recv, cond_send, cond_recv, row_send, row_recv, col_send, col_recv,
    load_sem, out_sem, near_sem,
):
    g, s, t = (lax.axis_index(name) for name in ("grp", "seq", "tile"))
    zl, c = g // 2, g % 2
    y, zh = s // 4, s % 4
    z = zh * 2 + zl
    sib = zl * 2 + (1 - c)
    head, working = (z + 8 - PLACE[0]) % 8, (z + 8 - PLACE[0]) % 8 < HEADS_TILE
    s_up, s_down = (s + 1) % 16, (s + 15) % 16

    def dev(grp, seq, tile=t):
        return {"grp": grp, "seq": seq, "tile": tile}

    def remote(src, dst, send, recv, to):
        return pltpu.make_async_remote_copy(
            src_ref=src, dst_ref=dst, send_sem=send, recv_sem=recv, device_id=to, device_id_type=MESH
        )

    def landed(ref, sem):
        pltpu.make_async_copy(ref, ref, sem).wait()

    partners = [dev(((z + i) % 8) % 2 * 2 + c, y * 4 + ((z + i) % 8) // 2) for i in range(1, 8)]
    partners += [dev(g, (y + i) % 4 * 4 + zh) for i in (1, 3)] + [dev(sib, s)]
    partners += [dev(g, s, (t + i) % 4) for i in range(1, 4)]
    barrier = pltpu.get_barrier_semaphore()
    for partner in partners:
        pl.semaphore_signal(barrier, inc=1, device_id=partner, device_id_type=MESH)
    pl.semaphore_wait(barrier, len(partners))

    first = ((k_hbm, k_buf.at[g, s]), (v_hbm, v_buf.at[g, s]), (q_hbm, q_buf.at[zl, zh]))

    def first_copy(i, h):
        src = first[i][0].at[:, h * HEAD:(h + 1) * HEAD]
        return remote(
            src, first[i][1], first_send.at[i, h], first_recv.at[i, zl, zh],
            dev(PLACE[h] % 2 * 2 + c, y * 4 + PLACE[h] // 2),
        )

    for i in range(3):
        for h in range(HEADS_TILE):
            @pl.when(z != PLACE[h])
            def _():
                first_copy(i, h).start()

            @pl.when(z == PLACE[h])
            def _():
                pltpu.make_async_copy(
                    first[i][0].at[:, h * HEAD:(h + 1) * HEAD], first[i][1], first_recv.at[i, zl, zh]
                ).start()

    loads = [
        pltpu.make_async_copy(src, dst, load_sem.at[i])
        for i, (src, dst) in enumerate((
            (stretch_hbm, stretch), (lat_hbm, lat.at[:, 32:96]), (wk_hbm, wk), (wv_hbm, wv), (wq_hbm, wq), (wb_hbm, wb),
        ))
    ]
    for load in loads:
        load.start()

    y_up, y_down, y_far = (y + 1) % 4, (y + 3) % 4, (y + 2) % 4
    for other in (y_up, y_down):
        pl.semaphore_signal(near_sem, inc=1, device_id=dev(g, other * 4 + zh), device_id_type=MESH)
    pl.semaphore_wait(near_sem, 2)

    mine, theirs = pl.ds(2 * c, 2), pl.ds(2 * (1 - c), 2)
    row_copies = [
        remote(lat_hbm.at[mine, 32:64], lat.at[mine, 0:32], row_send.at[0], row_recv.at[0], dev(g, s_up)),
        remote(lat_hbm.at[mine, 0:32], lat.at[mine, 96:128], row_send.at[1], row_recv.at[1], dev(g, s_down)),
    ]
    for copy in row_copies:
        copy.start()

    def project(refs, *pieces):
        cells = jnp.concatenate([lat[:, rows].reshape(-1, 1536) for rows in pieces], axis=0)
        wide = cells.astype(F32)
        squares = wide[:, :HEAD] * wide[:, :HEAD]
        for i in range(1, 12):
            lanes = slice(HEAD * i, HEAD * (i + 1))
            squares += wide[:, lanes] * wide[:, lanes]
        results = [(lat_sq, squares)] + [(ref, dot(cells, weight[...])) for weight, ref in refs]
        count = cells.shape[0] // len(pieces)
        for ref, result in results:
            for i, rows in enumerate(pieces):
                ref[:, rows] = result[count * i:count * (i + 1)].reshape(4, count // 4, -1)

    for load in loads[:5]:
        load.wait()
    project(((wk, lat_k), (wv, lat_v)), slice(32, 96))
    lat_q[...] = dot(lat[:, 32:96].reshape(256, 1536), wq[...]).reshape(4, 64, 384)

    bufs = (k_buf, v_buf)

    def region(kind, frame, row):
        return bufs[kind].at[frame, pl.ds(4 * row, 4)]

    def second(kind, frame, row, send, to):
        ref = region(kind, frame, row)
        return remote(ref, ref, send, second_recv.at[kind, frame, row], to)

    def low_of(i, frame):
        return jnp.where(stretch[frame] <= stretch[2 * i + c], 0.0, LOW)

    def score(row, core):
        for i in range(2):
            queries = q_buf[i].reshape(256, HEAD)
            top = m_ref[i]
            for part in range(2):
                frame = 2 * part + core
                keys = k_buf[frame, pl.ds(4 * row, 4)].reshape(256, HEAD)
                scores = lax.dot_general(queries, keys, NT, preferred_element_type=F32)
                s_buf[i, core * 4 + row, :, 256 * part:256 * (part + 1)] = scores
                top = jnp.maximum(top, jnp.maximum(scores[:, :HEAD], scores[:, HEAD:]) + low_of(i, frame))
            m_ref[i] = top

    def weigh(i):
        top = jnp.max(m_ref[i], axis=1, keepdims=True) * EXP2_SCALE
        m_ref[i] = jnp.broadcast_to(top, (256, HEAD))
        l_ref[i] = jnp.zeros((256, HEAD), F32)

        def block(j, carry):
            shift, total = m_ref[i], l_ref[i]
            for part in range(2):
                moved = shift - low_of(i, 2 * part + j // 4)
                for lane in range(2):
                    lanes = slice(256 * part + HEAD * lane, 256 * part + HEAD * (lane + 1))
                    weights = jnp.exp2(s_buf[i, j, :, lanes] * EXP2_SCALE - moved)
                    total += weights
                    w_buf[i, j, :, lanes] = weights.astype(BF16)
            l_ref[i] = total
            return carry

        lax.fori_loop(0, 8, block, 0)

    def blend(row, core):
        values = [v_buf[2 * part + core, pl.ds(4 * row, 4)].reshape(256, HEAD) for part in range(2)]
        values = jnp.concatenate(values, axis=0)
        for i in range(2):
            acc_ref[i] += dot(w_buf[i, core * 4 + row], values)

    def returned(i, j):
        return remote(o_buf.at[i, j], a_buf.at[head], ret_send.at[i, j], ret_recv.at[head], dev(2 * i + c, y * 4 + j))

    own_targets = [dev(g, y_up * 4 + zh), dev(g, y_down * 4 + zh), dev(sib, s)]
    far_rows = (y_down, y_up, y_far)

    def own_copy(kind, i, j):
        return second(kind, 2 * i + c, y, own_send.at[kind, i, j], own_targets[j])

    def forward_copy(kind, i):
        return second(kind, 2 * i + c, far_rows[i], fwd_send.at[kind, i], own_targets[i])

    def relay_copy(kind, i, j):
        return second(kind, 2 * i + c, far_rows[j], relay_send.at[j, kind, i], dev(sib, s))

    @pl.when(working)
    def _():
        m_ref[...] = jnp.full_like(m_ref, LOW)
        acc_ref[...] = jnp.zeros_like(acc_ref)

        for kind in range(2):
            for i in range(2):
                for j in range(4):
                    landed(bufs[kind].at[2 * i + c, 4 * y + j], first_recv.at[kind, i, j])
                own_copy(kind, i, i).start()
            for i, j in ((1, 0), (0, 1), (0, 2), (1, 2)):
                own_copy(kind, i, j).start()
        for i in range(2):
            for j in range(4):
                landed(q_buf.at[i, j], first_recv.at[2, i, j])

        def relay(kind, j):
            for i in range(2):
                landed(region(kind, 2 * i + c, far_rows[j]), second_recv.at[kind, 2 * i + c, far_rows[j]])
                if i == j:
                    forward_copy(kind, i).start()
                relay_copy(kind, i, j).start()

        def from_sibling(kind, row):
            for i in range(2):
                frame = 2 * i + 1 - c
                landed(region(kind, frame, row), second_recv.at[kind, frame, row])

        score(y, c)
        for j in range(2):
            relay(0, j)
        from_sibling(0, y)
        score(y, 1 - c)
        score(y_down, c)
        score(y_up, c)
        for j in range(2):
            relay(1, j)
        relay(0, 2)
        for row in (y_down, y_up):
            from_sibling(0, row)
            score(row, 1 - c)
        score(y_far, c)
        from_sibling(0, y_far)
        score(y_far, 1 - c)
        weigh(0)
        weigh(1)
        blend(y, c)
        from_sibling(1, y)
        blend(y, 1 - c)
        blend(y_down, c)
        blend(y_up, c)
        relay(1, 2)
        for row in (y_down, y_up):
            from_sibling(1, row)
            blend(row, 1 - c)
        blend(y_far, c)
        from_sibling(1, y_far)
        blend(y_far, 1 - c)

        for i in range(2):
            total = jnp.sum(l_ref[i], axis=1, keepdims=True)
            o_buf[i] = (acc_ref[i] / total).astype(BF16).reshape(4, 64, HEAD)
            for j in range(4):
                @pl.when(z != 2 * j + i)
                def _():
                    returned(i, j).start()

                @pl.when(z == 2 * j + i)
                def _():
                    pltpu.make_async_copy(o_buf.at[i, j], a_buf.at[head], ret_recv.at[head]).start()

    row_relays = []
    for i, rows in enumerate((slice(0, 32), slice(96, 128))):
        landed(lat.at[mine, rows], row_recv.at[i])
        ref = lat.at[mine, rows]
        row_relays.append(remote(ref, ref, row_send.at[2 + i], row_recv.at[2 + i], dev(sib, s)))
        row_relays[-1].start()
    for i, rows in enumerate((slice(0, 32), slice(96, 128))):
        landed(lat.at[theirs, rows], row_recv.at[2 + i])
    edge_id, cell = iota((32, 128), 0), iota((32, 128), 1)
    edge_cell = ((edge_id >> 1) & 7) * 16 + (edge_id & 1) + jnp.where(edge_id < 16, 14, 0)
    chosen = one_hot(edge_cell == cell)
    for frame in range(4):
        edges = dot(chosen, lat[frame, 0:128]).astype(BF16)
        edge_out[0, frame], edge_out[1, frame] = edges[:16], edges[16:]
    sides = (slice(128, 144), slice(144, 160))
    col_copies = [
        remote(edge_out.at[i], lat.at[:, sides[i]], col_send.at[i], col_recv.at[i], dev(g, s, neighbour))
        for i, neighbour in enumerate(((t + 1) % 4, (t + 3) % 4))
    ]
    for copy in col_copies:
        copy.start()
    project(((wk, lat_k), (wv, lat_v)), slice(0, 32), slice(96, 128))

    loads[5].wait()
    for h in range(HEADS_TILE):
        landed(a_buf.at[h], ret_recv.at[h])
    attended = jnp.concatenate([a_buf[h] for h in range(HEADS_TILE)], axis=1)
    row_id, token = iota((128, 64), 0), iota((128, 64), 1)
    tile_copies = []
    for offsets in ((2, 1), (3, 0)):
        tile = (t + jnp.where(row_id < 64, offsets[0], offsets[1])) & 3
        partial = jnp.zeros((128, 512), F32)
        for part in range(3):
            place = (row_id & 31) - 10 * part
            column = tile * 8 - 1 + place
            fits = (place >= 0) & (place < 10) & (column >= 0) & (column < 32)
            chosen = one_hot(fits & (((row_id >> 5) & 1) * 32 + column == token))
            rows = dot(chosen, attended).astype(BF16)
            partial += dot(rows, wb[:, 512 * part:512 * (part + 1)])
        for i, offset in enumerate(offsets):
            piece = partial[64 * i:64 * (i + 1)]
            if offset == 0:
                p_own[...] = piece
                continue
            slot = offset - 1
            p_send[slot] = piece.astype(BF16)
            tile_copies.append(remote(
                p_send.at[slot], p_recv.at[slot], tile_send.at[slot], tile_recv.at[slot], dev(g, s, (t + offset) % 4)
            ))
            tile_copies[-1].start()

    for i in range(3):
        landed(p_recv.at[i], tile_recv.at[i])
    summed = p_own[...]
    for i in range(3):
        summed += p_recv[i].astype(F32)
    squares = summed * summed
    squares = squares[:, :128] + squares[:, 128:256] + squares[:, 256:384] + squares[:, 384:]
    left, right = iota((64, 64), 0), iota((64, 64), 1)

    def token_of(row):
        place = row & 31
        return place - jnp.where(place >= 10, 10, 0) - jnp.where(place >= 20, 10, 0)

    same = ((left >> 5) == (right >> 5)) & (token_of(left) == token_of(right))
    together = jnp.dot(
        jnp.where(same, 1.0, 0.0), squares, preferred_element_type=F32, precision=lax.Precision.HIGHEST
    )
    mean = jnp.sum(together, axis=1, keepdims=True) * (1.0 / 1536)
    cond[g, 1:3] = (summed * lax.rsqrt(mean + EPS)).astype(BF16).reshape(2, 32, 512)

    slots = (slice(1, 3), slice(0, 1), slice(3, 4))

    def cond_copy(frame, src, slot, sem, to):
        return remote(cond.at[frame, src], cond.at[frame, slots[slot]], cond_send.at[sem], cond_recv.at[frame, slot], to)

    across = (1 - zl) * 2 + c
    cond_copies = [
        cond_copy(g, slots[0], 0, 0, dev(across, s)),
        cond_copy(g, slice(2, 3), 1, 1, dev(c, s_up)),
        cond_copy(g, slice(2, 3), 1, 2, dev(2 + c, s_up)),
        cond_copy(g, slice(1, 2), 2, 3, dev(c, s_down)),
        cond_copy(g, slice(1, 2), 2, 4, dev(2 + c, s_down)),
        cond_copy(g, slots[0], 0, 5, dev(sib, s)),
    ]
    for copy in cond_copies:
        copy.start()
    for i in range(2):
        landed(lat.at[:, sides[i]], col_recv.at[i])
    project(((wk, lat_k), (wv, lat_v)), slice(128, 160))
    arrivals = [((1 - zl) * 2 + c, 0), (c, 1), (2 + c, 1), (c, 2), (2 + c, 2)]
    for i, (frame, slot) in enumerate(arrivals):
        landed(cond.at[frame, slots[slot]], cond_recv.at[frame, slot])
        cond_copies.append(cond_copy(frame, slots[slot], slot, 6 + i, dev(sib, s)))
        cond_copies[-1].start()

    place, source = iota((64, 128), 0), iota((64, 128), 1)
    unpack = [
        one_hot(((place & 15) < 10) & ((place >> 4) * 32 + 10 * part + (place & 15) == source)) for part in range(3)
    ]
    cell, source = iota((160, 64), 0), iota((160, 64), 1)
    side = cell - 128
    cell_row = jnp.where(cell < 128, cell >> 4, (side >> 1) & 7)
    cell_token = jnp.where(cell < 128, 1 + ((cell & 15) >> 1), jnp.where(side < 16, 0, 9))
    above = (cell_row >> 1) * 16 + cell_token == source
    spread = one_hot(above)
    diagonal = iota((64, 64), 0) == iota((64, 64), 1)

    query, key = iota((64, 160), 0), iota((64, 160), 1)
    side = key - 128
    key_row = jnp.where(key < 128, key >> 4, (side >> 1) & 7)
    key_col = jnp.where(key < 128, 2 + (key & 15), (side & 1) + jnp.where(side < 16, 0, 18))
    row_off, col_off = key_row - (query >> 4) - 2, key_col - (query & 15) - 2
    row_at, col_at = 4 * s - 2 + key_row, 16 * t - 2 + key_col
    near = (jnp.abs(row_off) <= 2) & (jnp.abs(col_off) <= 2)
    near = near & (row_at >= 0) & (row_at < 64) & (col_at >= 0) & (col_at < 64)
    low = jnp.where(near, 0.0, LOW)

    def layer(core):
        for i in range(2):
            rows = cond[2 * i + core].reshape(128, 512)
            for part in range(3):
                tok[i, :, 512 * part:512 * (part + 1)] = dot(unpack[part], rows).astype(BF16)
        tokens = tok[...].reshape(128, 1536)
        parts = [dot(tokens, weight[...]).astype(BF16) for weight in (wk, wv, wq)]
        scores, blocks = [], []
        for i in range(2):
            frame = 2 * i + core
            pair = lax.dot_general(tok[i], tok[i], NT, preferred_element_type=F32)
            token_sq = jnp.sum(jnp.where(diagonal, pair, 0.0), axis=0, keepdims=True)
            cross = lax.dot_general(lat[frame], tok[i], NT, preferred_element_type=F32)
            square = jnp.sum(jnp.where(above, 2.0 * cross + token_sq, 0.0), axis=1, keepdims=True)
            square = jnp.maximum(square + jnp.sum(lat_sq[frame], axis=1, keepdims=True), 0.0)
            scale = lax.rsqrt(square * (1.0 / 1536) + EPS)
            keys, values = (
                (scale * (ref[frame] + dot(spread, part[64 * i:64 * (i + 1)]))).astype(BF16)
                for ref, part in ((lat_k, parts[0]), (lat_v, parts[1]))
            )
            queries = dot(spread[32:96], parts[2][64 * i:64 * (i + 1)])
            queries = (scale[32:96] * (lat_q[frame] + queries)).astype(BF16)
            for h in range(3):
                lanes = slice(h * HEAD, (h + 1) * HEAD)
                score = lax.dot_general(queries[:, lanes], keys[:, lanes], NT, preferred_element_type=F32)
                scores.append(score * HEAD ** (-0.5) + low)
                blocks.append((frame, lanes, values[:, lanes]))
        scores = jnp.concatenate(scores, axis=0)
        unscaled = jnp.exp(scores - jnp.max(scores, axis=1, keepdims=True))
        weights = (unscaled * (1.0 / jnp.sum(unscaled, axis=1, keepdims=True))).astype(BF16)
        for i, (frame, lanes, values) in enumerate(blocks):
            blended = dot(weights[64 * i:64 * (i + 1)], values).astype(BF16)
            out_buf[frame, :, :, lanes] = blended.reshape(4, 16, HEAD)

    layer(c)
    for frame, slot in [(sib, 0)] + [(2 * i + 1 - c, slot) for i, slot in ((0, 1), (1, 1), (0, 2), (1, 2))] + [((1 - zl) * 2 + 1 - c, 0)]:
        landed(cond.at[frame, slots[slot]], cond_recv.at[frame, slot])
    layer(1 - c)
    result = pltpu.make_async_copy(out_buf, out_hbm, out_sem)
    result.start()

    for i in range(3):
        for h in range(HEADS_TILE):
            @pl.when(z != PLACE[h])
            def _():
                first_copy(i, h).wait_send()
    @pl.when(working)
    def _():
        for kind in range(2):
            for i in range(2):
                for j in range(3):
                    own_copy(kind, i, j).wait_send()
                    relay_copy(kind, i, j).wait_send()
                forward_copy(kind, i).wait_send()
        for i in range(2):
            for j in range(4):
                @pl.when(z != 2 * j + i)
                def _():
                    returned(i, j).wait_send()

    for copy in row_copies + row_relays + tile_copies + col_copies + cond_copies:
        copy.wait_send()
    result.wait()


def local(base_q, base_k, base_v, frame_stretch, bridge_w, sr_latent, sr_wq, sr_wk, sr_wv):
    hbm = pl.BlockSpec(memory_space=pltpu.HBM)
    dma = pltpu.SemaphoreType.DMA
    vmem = pltpu.VMEM
    call = pl.pallas_call(
        kernel,
        out_shape=jax.ShapeDtypeStruct((4, 4, 16, 384), BF16),
        in_specs=[hbm] * 9,
        out_specs=hbm,
        scratch_shapes=[
            pltpu.SMEM((4,), jnp.int32),
            vmem((2, 4, 64, HEAD), BF16),
            vmem((4, 16, 64, HEAD), BF16),
            vmem((4, 16, 64, HEAD), BF16),
            vmem((2, 8, 256, 512), F32),
            vmem((2, 8, 256, 512), BF16),
            vmem((2, 256, HEAD), F32),
            vmem((2, 256, HEAD), F32),
            vmem((2, 256, HEAD), F32),
            vmem((2, 4, 64, HEAD), BF16),
            vmem((HEADS_TILE, 64, HEAD), BF16),
            vmem((768, 1536), BF16),
            vmem((1536, 384), BF16),
            vmem((1536, 384), BF16),
            vmem((1536, 384), BF16),
            vmem((4, 160, 1536), BF16),
            vmem((4, 160, HEAD), F32),
            vmem((4, 64, 384), F32),
            vmem((4, 160, 384), F32),
            vmem((4, 160, 384), F32),
            vmem((2, 4, 16, 1536), BF16),
            vmem((64, 512), F32),
            vmem((3, 64, 512), BF16),
            vmem((3, 64, 512), BF16),
            vmem((4, 4, 32, 512), BF16),
            vmem((2, 64, 1536), BF16),
            vmem((4, 4, 16, 384), BF16),
            dma((3, HEADS_TILE)),
            dma((3, 2, 4)),
            dma((2, 2, 3)),
            dma((2, 2)),
            dma((3, 2, 2)),
            dma((2, 4, 4)),
            dma((2, 4)),
            dma((HEADS_TILE,)),
            dma((3,)),
            dma((3,)),
            dma((11,)),
            dma((4, 3)),
            dma((4,)),
            dma((4,)),
            dma((2,)),
            dma((2,)),
            dma((6,)),
            dma,
            pltpu.SemaphoreType.REGULAR,
        ],
        compiler_params=pltpu.CompilerParams(
            collective_id=0, has_side_effects=True, vmem_limit_bytes=62 * 1024 * 1024
        ),
        cost_estimate=pl.CostEstimate(flops=4 * 10**9, bytes_accessed=16 * 2**20, transcendentals=2 * 10**6),
    )
    return call(
        base_q.reshape(64, 768), base_k.reshape(64, 768), base_v.reshape(64, 768), frame_stretch,
        bridge_w, sr_latent.reshape(4, 64, 1536), sr_wq, sr_wk, sr_wv,
    )


def solution(mesh):
    placed = (
        P("grp", "seq", None, "tile"),
        P("grp", "seq", None, "tile"),
        P("grp", "seq", None, "tile"),
        P(),
        P("tile", None),
        P(None, "seq", "tile", None),
        P(None, "grp"),
        P(None, "grp"),
        P(None, "grp"),
    )
    return jax.shard_map(
        local, mesh=mesh, in_specs=placed, out_specs=P(None, "seq", "tile", "grp"), check_vma=False
    )
```
